32 devices in a mesh: dp: 16 (over z, y, core), mp: 2 (over x).
Axes of the slice: x: 2, y: 2, z: 4, core: 2. Of those that a mesh axis runs over, the one named last changes fastest.
Arguments:
- hidden_state_rows: bfloat16 [8192, 8192], P('dp', 'mp'), may hold values from -6 to 6
- request_adapter_index: int32 [8192], P('dp'), may hold values from 0 to 15, as said below
- adapter_store_slot: int32 [16], replicated, may hold values from 0 to 15, as said below
- down_weight_store: bfloat16 [16, 4, 8192, 64], P('dp', None, 'mp'), may hold values from -0.0625 to 0.0625
- up_weight_store: bfloat16 [16, 4, 64, 8192], P('dp', None, None, 'mp'), may hold values from -0.75 to 0.75
Outputs:
- adapted_rows: bfloat16 [8192, 8192], P('dp', 'mp')
The draws below stay inside these ranges and needn't reach their ends.
Inputs may be any that keep to these rules, and one draw needn't show every extreme that they name: `request_adapter_index`: among the 512 requests of one index of dp no adapter is named more than 64 times; in every draw one adapter is named exactly 64 times by every index of dp. `adapter_store_slot`: each slot is used by exactly one adapter; slot s lies in store shard s.
All inputs are finite; a program needn't handle non-finite values.
Results may differ from the reference program's by a relative error of at most 0.0075.
Values may be sent and summed in bfloat16 or wider, within the bound.
No kernel may reach another device: no remote copies, remote signals or barrier semaphores. Data moves between devices by JAX's collectives and lax.ppermute only.
A program may use at most 64 MiB of HBM per device.

```python
import jax
import jax.numpy as jnp
from jax import lax

MODEL_WIDTH = 8192
ADAPTER_RANK = 64
LAYER_COUNT = 4
ADP_DEV = 1
TOK_DEV = 512
ADAPTER_COUNT = 16
MOST = 64
TOKENS = 8192
N_DP = 16


def route_tables(key):
    slot_of = jax.random.permutation(jax.random.fold_in(key, 11), ADAPTER_COUNT).astype(jnp.int32)
    owner_hot = jax.random.randint(jax.random.fold_in(key, 12), (), 0, ADAPTER_COUNT // ADP_DEV)
    adapter_at = jnp.argsort(slot_of, stable=True).astype(jnp.int32)
    return (slot_of, owner_hot, adapter_at)


def draw_adapter_store_slot(key, part):
    return route_tables(key)[0]


def draw_request_adapter_index(key, part):
    slot_of, owner_hot, adapter_at = route_tables(key)
    rolled = jnp.roll(adapter_at, -(owner_hot * ADP_DEV))
    hot_ones = rolled[:ADP_DEV]
    others = rolled[ADP_DEV:]
    spare = TOK_DEV - ADP_DEV * MOST
    n_others = ADAPTER_COUNT - ADP_DEV

    def one_block(block):
        block_key = jax.random.fold_in(jax.random.fold_in(key, 100), block)
        mixed = others[jax.random.permutation(jax.random.fold_in(block_key, 1), n_others)]
        head = jnp.repeat(hot_ones, MOST)
        tail = mixed[jnp.arange(spare, dtype=jnp.int32) % n_others]
        whole = jnp.concatenate([head, tail])
        return whole[jax.random.permutation(jax.random.fold_in(block_key, 2), TOK_DEV)]
    blocks = jax.vmap(one_block)(jnp.arange(N_DP, dtype=jnp.int32))
    return blocks.reshape(TOKENS).astype(jnp.int32)


def shard_levels(stream_key, dims, pieces, smallest, high):
    loudness = 1.0
    for axis_at, parts in pieces:
        draws = jax.random.uniform(jax.random.fold_in(jax.random.fold_in(stream_key, 6), axis_at), (parts,), jnp.float32, smallest / len(pieces), high / len(pieces))
        loudness = loudness * jnp.repeat(jnp.exp(draws), dims[axis_at] // parts).reshape((-1,) + (1,) * (len(dims) - 1 - axis_at))
    return loudness


def noise(rng, dims, spread, most, shards=(), kind=jnp.bfloat16):
    values = jax.random.normal(rng, dims, jnp.float32) * spread
    if len(shards) > 0:
        values = shard_levels(rng, dims, shards, -0.22, 0.18) * values
    return jnp.clip(values, min=-most, max=most).astype(kind)


def setup_inputs(seed: int = 0) -> dict:
    keys = jax.random.split(jax.random.key(seed), 6)
    return {
        "hidden_state_rows": noise(keys[0], (TOKENS, MODEL_WIDTH), 1.0, 6.0, ((0, 16), (1, 2))),
        "request_adapter_index": draw_request_adapter_index(jax.random.fold_in(keys[5], 71), 0),
        "adapter_store_slot": draw_adapter_store_slot(jax.random.fold_in(keys[5], 71), 0),
        "down_weight_store": noise(keys[3], (ADAPTER_COUNT, LAYER_COUNT, MODEL_WIDTH, ADAPTER_RANK), MODEL_WIDTH ** -0.5, 0.0625, ((0, 16), (2, 2))),
        "up_weight_store": noise(keys[4], (ADAPTER_COUNT, LAYER_COUNT, ADAPTER_RANK, MODEL_WIDTH), ADAPTER_RANK ** -0.5, 0.75, ((0, 16), (3, 2))),
    }


epsilon = 1e-05

def adapter_layer(current, down_a, up_b):
    widened = current.astype(jnp.float32)
    mean_sq = lax.optimization_barrier(jnp.mean(widened * widened, axis=-1, keepdims=True))
    reduced = (jnp.dot(current, down_a, preferred_element_type=jnp.float32) * lax.rsqrt(mean_sq + epsilon)).astype(jnp.bfloat16)
    return (widened + jnp.dot(reduced, up_b, preferred_element_type=jnp.float32)).astype(jnp.bfloat16)

def reference(hidden_state_rows, request_adapter_index, adapter_store_slot, down_weight_store, up_weight_store):
    bucket = N_DP * MOST
    by_adapter = jnp.argsort(request_adapter_index, stable=True).astype(jnp.int32)
    counts = jax.ops.segment_sum(jnp.ones((TOKENS,), jnp.int32), request_adapter_index, ADAPTER_COUNT).astype(jnp.int32)
    starts = (jnp.cumsum(counts) - counts).astype(jnp.int32)

    def per_adapter(result, adapter):
        offsets = jnp.arange(bucket, dtype=jnp.int32)
        is_live = offsets < counts[adapter]
        picked = by_adapter[jnp.minimum(starts[adapter] + offsets, TOKENS - 1)]
        current = hidden_state_rows[picked]
        request_slot_index = adapter_store_slot[adapter]
        down_projected = lax.dynamic_index_in_dim(down_weight_store, request_slot_index, 0, keepdims=False)
        up_projected = lax.dynamic_index_in_dim(up_weight_store, request_slot_index, 0, keepdims=False)
        for layer_index in range(LAYER_COUNT):
            current = adapter_layer(current, down_projected[layer_index], up_projected[layer_index])
        placed = jnp.where(is_live, picked, TOKENS).astype(jnp.int32)
        return (result.at[placed].set(current, mode='drop'), None)
    result, _ = lax.scan(per_adapter, jnp.zeros((TOKENS, MODEL_WIDTH), jnp.bfloat16), jnp.arange(ADAPTER_COUNT, dtype=jnp.int32))
    return result
```

```python
import jax
import jax.numpy as jnp
from jax import lax
from jax.sharding import PartitionSpec as P

epsilon = 1e-05
F32 = jnp.float32
BF16 = jnp.bfloat16


def sum_mp(value):
    size = lax.axis_size("mp")
    if size == 2:
        return value + lax.ppermute(value, "mp", [(0, 1), (1, 0)])
    return lax.psum(value, "mp")


def one_hot(rows, columns):
    return (rows[:, None] == columns[None, :]).astype(BF16)


def place(hot, values):
    return jnp.dot(hot, values, preferred_element_type=F32).astype(BF16)


def sketch_weights(down, up):
    layers, width, rank = down.shape
    flat_down = jnp.swapaxes(down, 1, 2).reshape(layers * rank, width)
    return jnp.concatenate([flat_down, up.reshape(layers * rank, width)], axis=0)


def against(left, right):
    return lax.dot_general(left, right, (((1,), (1,)), ((), ())), preferred_element_type=F32)


def gram(weights):
    half = weights.shape[0] // 2
    return sum_mp(against(weights[half:], weights))


def exact_dot(low, table):
    high = table.astype(BF16)
    rest = (table - high.astype(F32)).astype(BF16)
    return jnp.dot(low, high, preferred_element_type=F32) + jnp.dot(
        low, rest, preferred_element_type=F32
    )


def low_rank(sketch, squares, table, layers, model_width):
    total = sketch.shape[1] // 2
    rank = total // layers
    lows = []
    for layer in range(layers):
        here = slice(layer * rank, (layer + 1) * rank)
        there = slice(total + layer * rank, total + (layer + 1) * rank)
        projected, overlap = sketch[:, here], sketch[:, there]
        if lows:
            before = jnp.concatenate(lows, axis=1)
            rows = slice(0, layer * rank)
            projected = projected + exact_dot(before, table[rows, here])
            overlap = overlap + exact_dot(before, table[rows, there])
        low = (projected * lax.rsqrt(squares / model_width + epsilon)).astype(BF16)
        lows.append(low)
        step = 2.0 * overlap + exact_dot(low, table[here, there])
        squares = jnp.maximum(
            squares + jnp.sum(low.astype(F32) * step, axis=1, keepdims=True), 0.0
        )
    return jnp.concatenate(lows, axis=1)


def adapt(rows, weights, table, layers, model_width):
    widened = rows.astype(F32)
    squares = jnp.sum(widened * widened, axis=1, keepdims=True)
    sketch = sum_mp(against(rows, weights))
    squares = sum_mp(squares)
    low = low_rank(sketch, squares, table, layers, model_width)
    half = weights.shape[0] // 2
    update = jnp.dot(low, weights[half:], preferred_element_type=F32)
    return (widened + update).astype(BF16)


def local(hidden, request_adapter, store_slot, down_store, up_store):
    count, width = hidden.shape
    owners = lax.axis_size("dp")
    adapters = store_slot.shape[0]
    assert adapters == owners and down_store.shape[0] == 1
    layers = down_store.shape[1]
    model_width = width * lax.axis_size("mp")
    slot_rows = count // adapters
    chunks = 2 if slot_rows % 32 == 0 else 1
    chunk_rows = slot_rows // chunks
    group = 1
    while group * group < owners:
        group *= 2
    planes = owners // group
    me = lax.axis_index("dp")
    my_plane, my_place = me // group, me % group

    adapter_ids = jnp.arange(adapters, dtype=jnp.int32)
    matches = request_adapter[:, None] == adapter_ids[None, :]
    slot = jnp.sum(jnp.where(matches, store_slot[None, :], 0), axis=1)
    request_ids = jnp.arange(count, dtype=jnp.int32)
    earlier = (slot[:, None] == slot[None, :]) & (request_ids[:, None] > request_ids[None, :])
    position = jnp.sum(earlier.astype(jnp.int32), axis=1)
    by_slot = slot[:, None] == adapter_ids[None, :]
    counts = jnp.sum(by_slot.astype(jnp.int32), axis=0)
    excess = lax.psum(jnp.maximum(counts - slot_rows, 0), "dp")

    arrived = []
    targets = []
    for chunk in range(chunks):
        offset = position - chunk * chunk_rows
        target = jnp.where(
            (offset >= 0) & (offset < chunk_rows), slot * chunk_rows + offset, -1
        )
        targets.append(target)
        packed = place(one_hot(jnp.arange(owners * chunk_rows), target), hidden)
        arrived.append(
            lax.all_to_all(
                packed.reshape(owners, chunk_rows, width), "dp", 0, 0, tiled=True
            ).reshape(owners * chunk_rows, width)
        )

    weights = sketch_weights(down_store[0], up_store[0])
    piece_rows = weights.shape[0] // group
    pieces = weights.reshape(group, piece_rows, width)
    spread = []
    for step in range(group):
        piece = lax.dynamic_index_in_dim(pieces, my_place ^ step, 0, keepdims=False)
        if step:
            piece = lax.ppermute(piece, "dp", [(i, i ^ step) for i in range(owners)])
        spread.append(piece)
    chosen = jnp.argmax(excess.reshape(planes, group), axis=1).astype(jnp.int32)
    mine = lax.dynamic_index_in_dim(
        jnp.stack(spread), my_place ^ chosen[my_plane], 0, keepdims=False
    )
    groups = [[p * group + q for q in range(group)] for p in range(planes)]
    plane_weights = lax.all_gather(mine, "dp", axis_index_groups=groups, tiled=True)
    table = gram(weights)
    plane_table = gram(plane_weights)

    plane = slot // group
    is_chosen = slot % group == jnp.sum(
        jnp.where(plane[:, None] == jnp.arange(planes)[None, :], chosen[None, :], 0), axis=1
    )
    over = position >= slot_rows
    over_target = jnp.where(
        over & is_chosen, (plane ^ my_plane) * slot_rows + position - slot_rows, -1
    )
    over_packed = place(one_hot(jnp.arange(planes * slot_rows), over_target), hidden)

    def swap_planes(rows):
        blocks = rows.reshape(planes, slot_rows, width)
        moved = [blocks[0]]
        for step in range(1, planes):
            pairs = [(i, i ^ (step * group)) for i in range(owners)]
            moved.append(lax.ppermute(blocks[step], "dp", pairs))
        return jnp.concatenate(moved, axis=0)

    over_arrived = swap_planes(over_packed)

    returned = []
    for rows in arrived:
        done = adapt(rows, weights, table, layers, model_width)
        returned.append(
            lax.all_to_all(
                done.reshape(owners, chunk_rows, width), "dp", 0, 0, tiled=True
            ).reshape(owners * chunk_rows, width)
        )
    returned.append(
        swap_planes(adapt(over_arrived, plane_weights, plane_table, layers, model_width))
    )
    targets.append(over_target)
    result = jnp.zeros((count, width), F32)
    for rows, target in zip(returned, targets):
        hot = one_hot(target, jnp.arange(rows.shape[0]))
        result = result + jnp.dot(hot, rows, preferred_element_type=F32)
    result = result.astype(BF16)

    served = jnp.sum(
        jnp.where(
            adapter_ids[:, None] // group == jnp.arange(planes)[None, :], chosen[None, :], 0
        ),
        axis=1,
    ) == adapter_ids % group
    waiting = jnp.where(served, 0, excess) > 0
    order = jnp.cumsum(waiting.astype(jnp.int32)) - 1
    rounds = jnp.sum(waiting.astype(jnp.int32))

    def one_round(state):
        at, filled = state
        owner = jnp.sum(jnp.where(waiting & (order == at), adapter_ids, 0))
        own = jnp.where(me == owner, weights, jnp.zeros_like(weights))
        round_weights = lax.psum(own, "dp")
        target = jnp.where(over & (slot == owner), position - slot_rows, -1)
        rows = place(one_hot(jnp.arange(slot_rows), target), hidden)
        done = adapt(rows, round_weights, gram(round_weights), layers, model_width)
        back = place(one_hot(target, jnp.arange(slot_rows)), done)
        return at + 1, jnp.where((target >= 0)[:, None], back, filled)

    _, result = lax.while_loop(lambda state: state[0] < rounds, one_round, (0, result))
    return result


def solution(mesh):
    return jax.shard_map(
        local,
        mesh=mesh,
        in_specs=(
            P("dp", "mp"),
            P("dp"),
            P(),
            P("dp", None, "mp", None),
            P("dp", None, None, "mp"),
        ),
        out_specs=P("dp", "mp"),
        check_vma=False,
    )
```

```python
import math

import jax
import jax.numpy as jnp
import numpy as np
from jax import lax
from jax.experimental import pallas as pl
from jax.experimental.pallas import tpu as pltpu
from jax.sharding import PartitionSpec as P

epsilon = 1e-05
F32 = jnp.float32
BF16 = jnp.bfloat16
VMEM_BYTES = 40 * 2**20


def parts_mp(value):
    size = lax.axis_size("mp")
    if size == 2:
        return [value, lax.ppermute(value, "mp", [(0, 1), (1, 0)])]
    return [lax.psum(value, "mp")]


def whole(array):
    return pl.BlockSpec(array.shape, lambda step: (0,) * array.ndim)


def columns(rows, tile, part=0):
    return pl.BlockSpec((rows, tile), lambda step: (part, step))


def call(body, outs, out_specs, operands, in_specs, steps, scratch=(), aliases=None):
    return pl.pallas_call(
        body,
        grid=(steps,),
        out_shape=outs,
        in_specs=in_specs,
        out_specs=out_specs,
        scratch_shapes=list(scratch),
        input_output_aliases=aliases or {},
        compiler_params=pltpu.CompilerParams(vmem_limit_bytes=VMEM_BYTES),
        cost_estimate=pl.CostEstimate(flops=1, bytes_accessed=1, transcendentals=0),
    )(*operands)


def tiling(width):
    tile = math.gcd(width, 2048)
    return tile, width // tile


def pack(target, hidden, total):
    count, width = hidden.shape
    tile, steps = tiling(width)

    def body(target_ref, hidden_ref, out_ref):
        at = lax.broadcasted_iota(jnp.int32, (total, count), 0)
        hot = (at == target_ref[...]).astype(F32).astype(BF16)
        out_ref[...] = jnp.dot(hot, hidden_ref[...], preferred_element_type=F32).astype(BF16)

    target = target.reshape(1, count)
    return call(
        body,
        jax.ShapeDtypeStruct((total, width), BF16),
        columns(total, tile),
        (target, hidden),
        [whole(target), columns(count, tile)],
        steps,
    )


def unpack(targets, arrays):
    count = targets[0].shape[0]
    width = arrays[0].shape[1]
    tile, steps = tiling(width)

    def body(*refs):
        target_refs, array_refs, out_ref = refs[: len(arrays)], refs[len(arrays) : -1], refs[-1]
        total = jnp.zeros((count, tile), F32)
        for target_ref, array_ref in zip(target_refs, array_refs):
            at = lax.broadcasted_iota(jnp.int32, (count, array_ref.shape[0]), 1)
            hot = (at == target_ref[...]).astype(F32).astype(BF16)
            total = total + jnp.dot(hot, array_ref[...], preferred_element_type=F32)
        out_ref[...] = total.astype(BF16)

    targets = [target.reshape(count, 1) for target in targets]
    return call(
        body,
        jax.ShapeDtypeStruct((count, width), BF16),
        columns(count, tile),
        (*targets, *arrays),
        [whole(t) for t in targets] + [columns(a.shape[0], tile) for a in arrays],
        steps,
    )


def sketch_weights(down, up):
    layers, width, rank = down.shape
    flat_down = jnp.swapaxes(down, 1, 2).reshape(layers * rank, width)
    return jnp.concatenate([flat_down, up.reshape(layers * rank, width)], axis=0)


def against(left, right):
    return lax.dot_general(left, right, (((1,), (1,)), ((), ())), preferred_element_type=F32)


def gram(weights):
    total, width = weights.shape
    half = total // 2
    tile, steps = tiling(width)

    def body(weights_ref, out_ref):
        @pl.when(pl.program_id(0) == 0)
        def _():
            out_ref[...] = jnp.zeros_like(out_ref)

        out_ref[...] += against(weights_ref[half:, :], weights_ref[...])

    return call(
        body,
        jax.ShapeDtypeStruct((half, total), F32),
        pl.BlockSpec((half, total), lambda step: (0, 0)),
        (weights,),
        [columns(total, tile)],
        steps,
    )


def sketch(rows, weights, part=0, parts=1):
    count, width = rows.shape
    count //= parts
    total = weights.shape[0]
    tile, steps = tiling(width)

    def body(rows_ref, weights_ref, out_ref, narrow_ref):
        step = pl.program_id(0)

        @pl.when(step == 0)
        def _():
            out_ref[...] = jnp.zeros_like(out_ref)

        values = rows_ref[...]
        out_ref[:, :total] += against(values, weights_ref[...])
        widened = values.astype(F32)
        out_ref[:, total:] += jnp.sum(widened * widened, axis=1, keepdims=True)

        @pl.when(step == steps - 1)
        def _():
            narrow_ref[:, :total] = out_ref[:, :total].astype(BF16)
            squares = out_ref[:, total:]
            column = lax.broadcasted_iota(jnp.int32, squares.shape, 1)
            first = squares.astype(BF16).astype(F32)
            second = (squares - first).astype(BF16).astype(F32)
            third = squares - first - second
            terms = jnp.where(column == 0, first, jnp.where(column == 1, second, third))
            narrow_ref[:, total:] = jnp.where(column < 3, terms, 0.0).astype(BF16)

    shape = (count, total + 128)
    return call(
        body,
        [jax.ShapeDtypeStruct(shape, F32), jax.ShapeDtypeStruct(shape, BF16)],
        [pl.BlockSpec(shape, lambda step: (0, 0))] * 2,
        (rows, weights),
        [columns(count, tile, part), columns(total, tile)],
        steps,
    )


def sketch_parts(sketched, narrow):
    if lax.axis_size("mp") == 2:
        return [sketched, lax.ppermute(narrow, "mp", [(0, 1), (1, 0)])]
    return [lax.psum(sketched, "mp")]


def widen(part, total):
    if part.dtype == F32:
        return part
    part = part.astype(F32)
    squares = jnp.sum(part[:, total:], axis=1, keepdims=True)
    return jnp.concatenate([part[:, :total], jnp.broadcast_to(squares, part[:, total:].shape)], 1)


def low_rank(sketched, table, layers, model_width):
    half = table.shape[0]
    total = table.shape[1]
    rank = half // layers
    high = table.astype(BF16)
    rest = (table - high.astype(F32)).astype(BF16)
    projected, overlap = sketched[:, :half], sketched[:, half:total]
    squares = sketched[:, total : total + 1]
    column = lax.broadcasted_iota(jnp.int32, (sketched.shape[0], half), 1)
    low = jnp.zeros((sketched.shape[0], half), F32)
    added = jnp.zeros((sketched.shape[0], total), F32)
    for layer in range(layers):
        here = (column >= layer * rank) & (column < (layer + 1) * rank)
        scaled = (projected + added[:, :half]) * lax.rsqrt(squares / model_width + epsilon)
        scaled = scaled.astype(BF16).astype(F32)
        low = jnp.where(here, scaled, low)
        if layer + 1 < layers:
            narrow = low.astype(BF16)
            after = jnp.dot(narrow, high, preferred_element_type=F32) + jnp.dot(
                narrow, rest, preferred_element_type=F32
            )
            step = 2.0 * overlap + added[:, half:] + after[:, half:]
            change = jnp.sum(jnp.where(here, scaled * step, 0.0), axis=1, keepdims=True)
            squares = jnp.maximum(squares + change, 0.0)
            added = after
    return low.astype(BF16)


def finish(rows, sketched, tables, weights, layers, model_width, part=0, parts=1, filled=None):
    whole_count, width = rows.shape
    count = whole_count // parts
    half = weights.shape[0] // 2
    tile, steps = tiling(width)

    filled = [] if filled is None else [filled]

    def body(*refs):
        rows_ref, up_ref = refs[:2]
        sketch_refs = refs[2 : 2 + len(sketched)]
        table_refs = refs[2 + len(sketched) :][: len(tables)]
        out_ref, low_ref = refs[-2:]

        @pl.when(pl.program_id(0) == 0)
        def _():
            whole_sketch = sum(widen(ref[...], 2 * half) for ref in sketch_refs)
            whole_table = sum(ref[...] for ref in table_refs)
            low_ref[...] = low_rank(whole_sketch, whole_table, layers, model_width)

        update = jnp.dot(low_ref[...], up_ref[...], preferred_element_type=F32)
        out_ref[...] = (rows_ref[...].astype(F32) + update).astype(BF16)

    return call(
        body,
        jax.ShapeDtypeStruct((whole_count, width), BF16),
        columns(count, tile, part),
        (rows, weights, *sketched, *tables, *filled),
        [columns(count, tile, part), columns(half, tile, 1)]
        + [whole(a) for a in (*sketched, *tables)]
        + [pl.BlockSpec(memory_space=pl.ANY) for _ in filled],
        steps,
        scratch=[pltpu.VMEM((count, half), BF16)],
        aliases={2 + len(sketched) + len(tables): 0} if filled else None,
    )


def adapt(rows, weights, tables, layers, model_width):
    sketched = sketch_parts(*sketch(rows, weights))
    return finish(rows, sketched, tables, weights, layers, model_width)


def local(hidden, request_adapter, store_slot, down_store, up_store):
    count, width = hidden.shape
    owners = lax.axis_size("dp")
    adapters = store_slot.shape[0]
    assert adapters == owners and down_store.shape[0] == 1
    layers = down_store.shape[1]
    model_width = width * lax.axis_size("mp")
    slot_rows = count // adapters
    group = 1
    while group * group < owners:
        group *= 2
    planes = owners // group
    me = lax.axis_index("dp")
    my_plane, my_place = me // group, me % group

    adapter_ids = jnp.arange(adapters, dtype=jnp.int32)
    matches = request_adapter[:, None] == adapter_ids[None, :]
    slot = jnp.sum(jnp.where(matches, store_slot[None, :], 0), axis=1)
    request_ids = jnp.arange(count, dtype=jnp.int32)
    earlier = (slot[:, None] == slot[None, :]) & (request_ids[:, None] > request_ids[None, :])
    position = jnp.sum(earlier.astype(jnp.int32), axis=1)
    by_slot = slot[:, None] == adapter_ids[None, :]
    counts = jnp.sum(by_slot.astype(jnp.int32), axis=0)
    over = position >= slot_rows
    excess = jnp.maximum(counts - slot_rows, 0)

    plane = slot // group
    my_choice = jnp.argmax(excess.reshape(planes, group), axis=1).astype(jnp.int32)

    is_mine = jnp.sum(
        jnp.where(adapter_ids[:, None] // group == jnp.arange(planes)[None, :], my_choice, 0), axis=1
    ) == adapter_ids % group
    row_is_mine = jnp.any(by_slot & is_mine[None, :], axis=1)

    def add_over(value, steps):
        pairs = [[(i, i ^ step) for i in range(owners)] for step in steps]
        return value + sum(lax.ppermute(value, "dp", p) for p in pairs)

    def exchange(rows):
        blocks = rows.reshape(owners, slot_rows, width)
        return lax.all_to_all(blocks, "dp", 0, 0, tiled=True).reshape(owners * slot_rows, width)

    target = jnp.where(over, -1, slot * slot_rows + position)
    packed = pack(target, hidden, owners * slot_rows)
    tallies = add_over(jnp.stack([excess, jnp.where(is_mine, 0, excess)]), range(1, group))
    packed, tallies = lax.optimization_barrier((packed, tallies))
    arrived = exchange(packed)

    over_target = jnp.where(
        over & row_is_mine, (plane ^ my_plane) * slot_rows + position - slot_rows, -1
    )
    over_packed = pack(over_target, hidden, planes * slot_rows)

    weights = sketch_weights(down_store[0], up_store[0])
    table = parts_mp(gram(weights))

    plane_excess = tallies[0].reshape(planes, group)
    choice = jnp.argmax(
        lax.dynamic_index_in_dim(plane_excess, my_plane, 0, keepdims=False)
    ).astype(jnp.int32)
    is_choice = adapter_ids == my_plane * group + choice
    tallies = jnp.concatenate([tallies, is_choice.astype(jnp.int32)[None, :]])
    mine = weights
    rows_left = weights.shape[0] // group
    step = 1
    while step < group:
        my_bit = (my_place // step) % 2
        halves = mine.reshape(-1, 2, rows_left, width)
        keep = lax.dynamic_index_in_dim(halves, my_bit, 1, keepdims=False)
        give = lax.dynamic_index_in_dim(halves, 1 - my_bit, 1, keepdims=False)
        taken = lax.ppermute(give, "dp", [(i, i ^ step) for i in range(owners)])
        mine = jnp.where((choice // step) % 2 == my_bit, keep, taken)
        step *= 2
    mine = mine.reshape(rows_left, width)
    mine, tallies = lax.optimization_barrier((mine, tallies))
    tallies = add_over(tallies, range(group, owners, group))
    mine, tallies, over_packed, arrived, *table = lax.optimization_barrier(
        (mine, tallies, over_packed, arrived, *table)
    )

    groups = [[p * group + q for q in range(group)] for p in range(planes)]
    plane_weights = lax.all_gather(mine, "dp", axis_index_groups=groups, tiled=True)

    def swap_planes(rows):
        blocks = rows.reshape(planes, slot_rows, width)
        moved = [blocks[0]]
        for step in range(1, planes):
            pairs = [(i, i ^ (step * group)) for i in range(owners)]
            moved.append(lax.ppermute(blocks[step], "dp", pairs))
        return moved

    sketched, narrow = sketch(arrived, weights)
    narrow, over_packed = lax.optimization_barrier((narrow, over_packed))
    sketched = sketch_parts(sketched, narrow)
    over_arrived = swap_planes(over_packed)
    *over_arrived, sketched[0] = lax.optimization_barrier((*over_arrived, sketched[0]))
    done = finish(arrived, sketched, table, weights, layers, model_width)

    returned = [exchange(done)]
    plane_weights, over_arrived[0], done = lax.optimization_barrier(
        (plane_weights, over_arrived[0], done)
    )
    plane_table = parts_mp(gram(plane_weights))
    over_done = adapt(
        jnp.concatenate(over_arrived), plane_weights, plane_table, layers, model_width
    )

    excess, stayed, chosen = tallies
    shared = jnp.argmax(excess * chosen).astype(jnp.int32)

    def back_from(source):
        def moved(rows):
            blocks = rows.reshape(planes, slot_rows, width)
            got = [jnp.where(my_plane == source, blocks[0], jnp.zeros_like(blocks[0]))]
            for step in range(1, planes):
                pairs = [(source * group + q, (source ^ step) * group + q) for q in range(group)]
                got.append(lax.ppermute(blocks[step], "dp", pairs))
            return sum(got)

        return moved

    returned.append(
        lax.switch(shared // group, [back_from(source) for source in range(planes)], over_done)
    )
    over_target = jnp.where(
        over & row_is_mine & (slot == shared), position - slot_rows, -1
    )
    waiting = jnp.where(adapter_ids == shared, stayed, excess) > 0
    targets = [target, over_target]
    result = unpack(targets, returned)

    order = jnp.cumsum(waiting.astype(jnp.int32)) - 1
    rounds = jnp.sum(waiting.astype(jnp.int32))

    def one_round(state):
        at, filled = state
        owner = jnp.sum(jnp.where(waiting & (order == at), adapter_ids, 0))
        own = jnp.where(me == owner, weights, jnp.zeros_like(weights))
        round_weights = lax.psum(own, "dp")
        left = over & (slot == owner) & (over_target < 0)
        target = jnp.where(left, position - slot_rows, -1)
        rows = pack(target, hidden, slot_rows)
        round_table = parts_mp(gram(round_weights))
        done = adapt(rows, round_weights, round_table, layers, model_width)
        back = unpack([target], [done])
        return at + 1, jnp.where((target >= 0)[:, None], back, filled)

    _, result = lax.while_loop(lambda state: state[0] < rounds, one_round, (0, result))
    return result


def solution(mesh):
    return jax.shard_map(
        local,
        mesh=mesh,
        in_specs=(
            P("dp", "mp"),
            P("dp"),
            P(),
            P("dp", None, "mp", None),
            P("dp", None, None, "mp"),
        ),
        out_specs=P("dp", "mp"),
        check_vma=False,
    )
```

```python
import math

import jax
import jax.numpy as jnp
import numpy as np
from jax import lax
from jax.experimental import pallas as pl
from jax.experimental.pallas import tpu as pltpu
from jax.sharding import PartitionSpec as P

epsilon = 1e-05
F32 = jnp.float32
BF16 = jnp.bfloat16


def parts_mp(value):
    size = lax.axis_size("mp")
    if size == 2:
        return [value, lax.ppermute(value, "mp", [(0, 1), (1, 0)])]
    return [lax.psum(value, "mp")]


def tiling(width):
    tile = math.gcd(width, 1024)
    return [pl.ds(step * tile, tile) for step in range(width // tile)]


def call(body, outs, operands, streamed, scratch, vmem=40):
    in_specs = [
        pl.BlockSpec(memory_space=pl.ANY if step in streamed else pltpu.VMEM)
        for step in range(len(operands))
    ]
    out_specs = [
        pl.BlockSpec(memory_space=pltpu.HBM if wide else pltpu.VMEM) for _, wide in outs
    ]
    return pl.pallas_call(
        body,
        out_shape=[out for out, _ in outs],
        in_specs=in_specs,
        out_specs=out_specs,
        scratch_shapes=list(scratch),
        compiler_params=pltpu.CompilerParams(vmem_limit_bytes=vmem * 2**20),
        cost_estimate=pl.CostEstimate(flops=1, bytes_accessed=1, transcendentals=0),
    )(*operands)


def start_all(sources, targets, sems, tiles):
    copies = []
    for step, at in enumerate(tiles):
        copies.append([])
        for number, (source, target) in enumerate(zip(sources, targets)):
            copy = pltpu.make_async_copy(
                source.at[:, at], target.at[:, at], sems.at[number, step]
            )
            copy.start()
            copies[-1].append(copy)
    return copies


def wait_all(copies):
    for copy in copies:
        copy.wait()


def pack(target, hidden, total):
    count, width = hidden.shape
    tiles = tiling(width)

    def body(target_ref, hidden_ref, out_ref, hidden_buf, out_buf, in_sems, out_sems):
        copies = start_all([hidden_ref], [hidden_buf], in_sems, tiles)
        at = lax.broadcasted_iota(jnp.int32, (total, count), 0)
        hot = (at == target_ref[...]).astype(F32).astype(BF16)
        sent = []
        for step, tile in enumerate(tiles):
            wait_all(copies[step])
            out_buf[:, tile] = jnp.dot(
                hot, hidden_buf[:, tile], preferred_element_type=F32
            ).astype(BF16)
            sent.append(
                pltpu.make_async_copy(
                    out_buf.at[:, tile], out_ref.at[:, tile], out_sems.at[0, step]
                )
            )
            sent[-1].start()
        wait_all(sent)

    return call(
        body,
        [(jax.ShapeDtypeStruct((total, width), BF16), True)],
        (target.reshape(1, count), hidden),
        [1],
        [
            pltpu.VMEM((count, width), BF16),
            pltpu.VMEM((total, width), BF16),
            pltpu.SemaphoreType.DMA((1, len(tiles))),
            pltpu.SemaphoreType.DMA((1, len(tiles))),
        ],
        vmem=60,
    )[0]


def unpack(targets, arrays):
    count = targets[0].shape[0]
    width = arrays[0].shape[1]
    tiles = tiling(width)
    kinds = len(arrays)

    def body(*refs):
        target_refs, array_refs, out_ref = refs[:kinds], refs[kinds : 2 * kinds], refs[2 * kinds]
        buffers, out_buf, in_sems, out_sems = refs[2 * kinds + 1 : -3], *refs[-3:]
        copies = start_all(array_refs, buffers, in_sems, tiles)
        hots = []
        for target_ref, array_ref in zip(target_refs, array_refs):
            at = lax.broadcasted_iota(jnp.int32, (count, array_ref.shape[0]), 1)
            hots.append((at == target_ref[...]).astype(F32).astype(BF16))
        sent = []
        for step, tile in enumerate(tiles):
            wait_all(copies[step])
            total = sum(
                jnp.dot(hot, buffer[:, tile], preferred_element_type=F32)
                for hot, buffer in zip(hots, buffers)
            )
            out_buf[:, tile] = total.astype(BF16)
            sent.append(
                pltpu.make_async_copy(
                    out_buf.at[:, tile], out_ref.at[:, tile], out_sems.at[0, step]
                )
            )
            sent[-1].start()
        wait_all(sent)

    return call(
        body,
        [(jax.ShapeDtypeStruct((count, width), BF16), True)],
        (*[target.reshape(count, 1) for target in targets], *arrays),
        range(kinds, 2 * kinds),
        [pltpu.VMEM(array.shape, BF16) for array in arrays]
        + [
            pltpu.VMEM((count, width), BF16),
            pltpu.SemaphoreType.DMA((kinds, len(tiles))),
            pltpu.SemaphoreType.DMA((1, len(tiles))),
        ],
    )[0]


def sketch_weights(down, up):
    layers, width, rank = down.shape
    flat_down = jnp.swapaxes(down, 1, 2).reshape(layers * rank, width)
    return jnp.concatenate([flat_down, up.reshape(layers * rank, width)], axis=0)


def against(left, right):
    return lax.dot_general(left, right, (((1,), (1,)), ((), ())), preferred_element_type=F32)


def gram(weights):
    total, width = weights.shape
    half = total // 2
    tiles = tiling(width)

    def body(weights_ref, out_ref, weights_buf, sems):
        copies = start_all([weights_ref], [weights_buf], sems, tiles)
        for step, tile in enumerate(tiles):
            wait_all(copies[step])
            values = weights_buf[:, tile]
            product = against(values[half:], values)
            out_ref[...] = product if step == 0 else out_ref[...] + product

    return call(
        body,
        [(jax.ShapeDtypeStruct((half, total), F32), False)],
        (weights,),
        [0],
        [pltpu.VMEM((total, width), BF16), pltpu.SemaphoreType.DMA((1, len(tiles)))],
    )[0]


def sketch(rows, weights):
    count, width = rows.shape
    total = weights.shape[0]
    tiles = tiling(width)

    def body(rows_ref, weights_ref, out_ref, narrow_ref, rows_buf, weights_buf, sems):
        copies = start_all([rows_ref, weights_ref], [rows_buf, weights_buf], sems, tiles)
        for step, tile in enumerate(tiles):
            wait_all(copies[step])
            values = rows_buf[:, tile]
            product = against(values, weights_buf[:, tile])
            widened = values.astype(F32)
            squares = jnp.broadcast_to(
                jnp.sum(widened * widened, axis=1, keepdims=True), (count, 128)
            )
            if step == 0:
                out_ref[:, :total] = product
                out_ref[:, total:] = squares
            else:
                out_ref[:, :total] += product
                out_ref[:, total:] += squares
        narrow_ref[:, :total] = out_ref[:, :total].astype(BF16)
        squares = out_ref[:, total:]
        column = lax.broadcasted_iota(jnp.int32, squares.shape, 1)
        first = squares.astype(BF16).astype(F32)
        second = (squares - first).astype(BF16).astype(F32)
        third = squares - first - second
        terms = jnp.where(column == 0, first, jnp.where(column == 1, second, third))
        narrow_ref[:, total:] = jnp.where(column < 3, terms, 0.0).astype(BF16)

    shape = (count, total + 128)
    return call(
        body,
        [(jax.ShapeDtypeStruct(shape, F32), False), (jax.ShapeDtypeStruct(shape, BF16), False)],
        (rows, weights),
        [0, 1],
        [
            pltpu.VMEM((count, width), BF16),
            pltpu.VMEM((total, width), BF16),
            pltpu.SemaphoreType.DMA((2, len(tiles))),
        ],
    )


def sketch_parts(sketched, narrow):
    if lax.axis_size("mp") == 2:
        return [sketched, lax.ppermute(narrow, "mp", [(0, 1), (1, 0)])]
    return [lax.psum(sketched, "mp")]


def widen(part, total):
    if part.dtype == F32:
        return part
    part = part.astype(F32)
    squares = jnp.sum(part[:, total:], axis=1, keepdims=True)
    return jnp.concatenate([part[:, :total], jnp.broadcast_to(squares, part[:, total:].shape)], 1)


def low_rank(sketched, table, layers, model_width):
    half = table.shape[0]
    total = table.shape[1]
    rank = half // layers
    high = table.astype(BF16)
    rest = (table - high.astype(F32)).astype(BF16)
    projected, overlap = sketched[:, :half], sketched[:, half:total]
    squares = sketched[:, total : total + 1]
    column = lax.broadcasted_iota(jnp.int32, (sketched.shape[0], half), 1)
    low = jnp.zeros((sketched.shape[0], half), F32)
    added = jnp.zeros((sketched.shape[0], total), F32)
    for layer in range(layers):
        here = (column >= layer * rank) & (column < (layer + 1) * rank)
        scaled = (projected + added[:, :half]) * lax.rsqrt(squares / model_width + epsilon)
        scaled = scaled.astype(BF16).astype(F32)
        low = jnp.where(here, scaled, low)
        if layer + 1 < layers:
            narrow = low.astype(BF16)
            after = jnp.dot(narrow, high, preferred_element_type=F32) + jnp.dot(
                narrow, rest, preferred_element_type=F32
            )
            step = 2.0 * overlap + added[:, half:] + after[:, half:]
            change = jnp.sum(jnp.where(here, scaled * step, 0.0), axis=1, keepdims=True)
            squares = jnp.maximum(squares + change, 0.0)
            added = after
    return low.astype(BF16)


def finish(rows, sketched, tables, weights, layers, model_width):
    count, width = rows.shape
    half = weights.shape[0] // 2
    tiles = tiling(width)

    def body(*refs):
        rows_ref, weights_ref = refs[:2]
        sketch_refs = refs[2 : 2 + len(sketched)]
        table_refs = refs[2 + len(sketched) :][: len(tables)]
        out_ref, rows_buf, up_buf, out_buf, in_sems, out_sems = refs[-6:]
        up_ref = weights_ref.at[pl.ds(half, half), :]
        copies = start_all([rows_ref, up_ref], [rows_buf, up_buf], in_sems, tiles)
        whole_sketch = sum(widen(ref[...], 2 * half) for ref in sketch_refs)
        whole_table = sum(ref[...] for ref in table_refs)
        low = low_rank(whole_sketch, whole_table, layers, model_width)
        sent = []
        for step, tile in enumerate(tiles):
            wait_all(copies[step])
            update = jnp.dot(low, up_buf[:, tile], preferred_element_type=F32)
            out_buf[:, tile] = (rows_buf[:, tile].astype(F32) + update).astype(BF16)
            sent.append(
                pltpu.make_async_copy(
                    out_buf.at[:, tile], out_ref.at[:, tile], out_sems.at[0, step]
                )
            )
            sent[-1].start()
        wait_all(sent)

    return call(
        body,
        [(jax.ShapeDtypeStruct((count, width), BF16), True)],
        (rows, weights, *sketched, *tables),
        [0, 1],
        [
            pltpu.VMEM((count, width), BF16),
            pltpu.VMEM((half, width), BF16),
            pltpu.VMEM((count, width), BF16),
            pltpu.SemaphoreType.DMA((2, len(tiles))),
            pltpu.SemaphoreType.DMA((1, len(tiles))),
        ],
        vmem=60,
    )[0]


def adapt(rows, weights, tables, layers, model_width):
    sketched = sketch_parts(*sketch(rows, weights))
    return finish(rows, sketched, tables, weights, layers, model_width)


def local(hidden, request_adapter, store_slot, down_store, up_store):
    count, width = hidden.shape
    owners = lax.axis_size("dp")
    adapters = store_slot.shape[0]
    assert adapters == owners and down_store.shape[0] == 1
    layers = down_store.shape[1]
    model_width = width * lax.axis_size("mp")
    slot_rows = count // adapters
    group = 1
    while group * group < owners:
        group *= 2
    planes = owners // group
    me = lax.axis_index("dp")
    my_plane, my_place = me // group, me % group

    adapter_ids = jnp.arange(adapters, dtype=jnp.int32)
    matches = request_adapter[:, None] == adapter_ids[None, :]
    slot = jnp.sum(jnp.where(matches, store_slot[None, :], 0), axis=1)
    request_ids = jnp.arange(count, dtype=jnp.int32)
    earlier = (slot[:, None] == slot[None, :]) & (request_ids[:, None] > request_ids[None, :])
    position = jnp.sum(earlier.astype(jnp.int32), axis=1)
    by_slot = slot[:, None] == adapter_ids[None, :]
    counts = jnp.sum(by_slot.astype(jnp.int32), axis=0)
    over = position >= slot_rows
    excess = jnp.maximum(counts - slot_rows, 0)

    plane = slot // group
    my_choice = jnp.argmax(excess.reshape(planes, group), axis=1).astype(jnp.int32)

    is_mine = jnp.sum(
        jnp.where(adapter_ids[:, None] // group == jnp.arange(planes)[None, :], my_choice, 0), axis=1
    ) == adapter_ids % group
    row_is_mine = jnp.any(by_slot & is_mine[None, :], axis=1)

    def add_over(value, steps):
        pairs = [[(i, i ^ step) for i in range(owners)] for step in steps]
        return value + sum(lax.ppermute(value, "dp", p) for p in pairs)

    def exchange(rows):
        blocks = rows.reshape(owners, slot_rows, width)
        return lax.all_to_all(blocks, "dp", 0, 0, tiled=True).reshape(owners * slot_rows, width)

    target = jnp.where(over, -1, slot * slot_rows + position)
    packed = pack(target, hidden, owners * slot_rows)
    tallies = add_over(jnp.stack([excess, jnp.where(is_mine, 0, excess)]), range(1, group))
    packed, tallies = lax.optimization_barrier((packed, tallies))
    arrived = exchange(packed)

    over_target = jnp.where(
        over & row_is_mine, (plane ^ my_plane) * slot_rows + position - slot_rows, -1
    )
    over_packed = pack(over_target, hidden, planes * slot_rows)

    weights = sketch_weights(down_store[0], up_store[0])
    table = parts_mp(gram(weights))

    plane_excess = tallies[0].reshape(planes, group)
    choice = jnp.argmax(
        lax.dynamic_index_in_dim(plane_excess, my_plane, 0, keepdims=False)
    ).astype(jnp.int32)
    is_choice = adapter_ids == my_plane * group + choice
    tallies = jnp.concatenate([tallies, is_choice.astype(jnp.int32)[None, :]])
    mine = weights
    rows_left = weights.shape[0] // group
    step = 1
    while step < group:
        my_bit = (my_place // step) % 2
        halves = mine.reshape(-1, 2, rows_left, width)
        keep = lax.dynamic_index_in_dim(halves, my_bit, 1, keepdims=False)
        give = lax.dynamic_index_in_dim(halves, 1 - my_bit, 1, keepdims=False)
        taken = lax.ppermute(give, "dp", [(i, i ^ step) for i in range(owners)])
        mine = jnp.where((choice // step) % 2 == my_bit, keep, taken)
        step *= 2
    mine = mine.reshape(rows_left, width)
    mine, tallies = lax.optimization_barrier((mine, tallies))
    tallies = add_over(tallies, range(group, owners, group))

    over_blocks = over_packed.reshape(planes, slot_rows, width)

    def to_plane(step, block):
        return lax.ppermute(block, "dp", [(i, i ^ (step * group)) for i in range(owners)])

    over_arrived = [over_blocks[0]] + [to_plane(step, over_blocks[step]) for step in range(1, 2)]
    mine, tallies, over_blocks, arrived, *rest = lax.optimization_barrier(
        (mine, tallies, over_blocks, arrived, *over_arrived, *table)
    )
    over_arrived, table = rest[: len(over_arrived)], rest[len(over_arrived) :]

    groups = [[p * group + q for q in range(group)] for p in range(planes)]
    plane_weights = lax.all_gather(mine, "dp", axis_index_groups=groups, tiled=True)

    sketched, narrow = sketch(arrived, weights)
    sketched = sketch_parts(sketched, narrow)
    later = [to_plane(step, over_blocks[step]) for step in range(2, planes)]
    *later[:-1], sketched[0] = lax.optimization_barrier((*later[:-1], sketched[0]))
    done = finish(arrived, sketched, table, weights, layers, model_width)
    *later, done = lax.optimization_barrier((*later, done))
    over_arrived = over_arrived + later

    returned = [exchange(done)]
    plane_weights, over_arrived[0], done = lax.optimization_barrier(
        (plane_weights, over_arrived[0], done)
    )
    plane_table = parts_mp(gram(plane_weights))
    over_done = adapt(
        jnp.concatenate(over_arrived), plane_weights, plane_table, layers, model_width
    )

    excess, stayed, chosen = tallies
    shared = jnp.argmax(excess * chosen).astype(jnp.int32)

    def back_from(source):
        def moved(rows):
            blocks = rows.reshape(planes, slot_rows, width)
            got = [jnp.where(my_plane == source, blocks[0], jnp.zeros_like(blocks[0]))]
            for step in range(1, planes):
                pairs = [(source * group + q, (source ^ step) * group + q) for q in range(group)]
                got.append(lax.ppermute(blocks[step], "dp", pairs))
            return sum(got)

        return moved

    returned.append(
        lax.switch(shared // group, [back_from(source) for source in range(planes)], over_done)
    )
    over_target = jnp.where(
        over & row_is_mine & (slot == shared), position - slot_rows, -1
    )
    waiting = jnp.where(adapter_ids == shared, stayed, excess) > 0
    targets = [target, over_target]
    result = unpack(targets, returned)

    order = jnp.cumsum(waiting.astype(jnp.int32)) - 1
    rounds = jnp.sum(waiting.astype(jnp.int32))

    def one_round(state):
        at, filled = state
        owner = jnp.sum(jnp.where(waiting & (order == at), adapter_ids, 0))
        own = jnp.where(me == owner, weights, jnp.zeros_like(weights))
        round_weights = lax.psum(own, "dp")
        left = over & (slot == owner) & (over_target < 0)
        target = jnp.where(left, position - slot_rows, -1)
        rows = pack(target, hidden, slot_rows)
        round_table = parts_mp(gram(round_weights))
        done = adapt(rows, round_weights, round_table, layers, model_width)
        back = unpack([target], [done])
        return at + 1, jnp.where((target >= 0)[:, None], back, filled)

    _, result = lax.while_loop(lambda state: state[0] < rounds, one_round, (0, result))
    return result


def solution(mesh):
    return jax.shard_map(
        local,
        mesh=mesh,
        in_specs=(
            P("dp", "mp"),
            P("dp"),
            P(),
            P("dp", None, "mp", None),
            P("dp", None, None, "mp"),
        ),
        out_specs=P("dp", "mp"),
        check_vma=False,
    )
```

```python
import math

import jax
import jax.numpy as jnp
import numpy as np
from jax import lax
from jax.experimental import pallas as pl
from jax.experimental.pallas import tpu as pltpu
from jax.sharding import PartitionSpec as P

epsilon = 1e-05
F32 = jnp.float32
BF16 = jnp.bfloat16


def parts_mp(value):
    size = lax.axis_size("mp")
    if size == 2:
        return [value, lax.ppermute(value, "mp", [(0, 1), (1, 0)])]
    return [lax.psum(value, "mp")]


def tiling(width):
    tile = math.gcd(width, 1024)
    return [pl.ds(step * tile, tile) for step in range(width // tile)]


def call(body, outs, operands, streamed, scratch, vmem=40):
    in_specs = [
        pl.BlockSpec(memory_space=pl.ANY if step in streamed else pltpu.VMEM)
        for step in range(len(operands))
    ]
    out_specs = [
        pl.BlockSpec(memory_space=pltpu.HBM if wide else pltpu.VMEM) for _, wide in outs
    ]
    return pl.pallas_call(
        body,
        out_shape=[out for out, _ in outs],
        in_specs=in_specs,
        out_specs=out_specs,
        scratch_shapes=list(scratch),
        compiler_params=pltpu.CompilerParams(vmem_limit_bytes=vmem * 2**20),
        cost_estimate=pl.CostEstimate(flops=1, bytes_accessed=1, transcendentals=0),
    )(*operands)


def start_all(sources, targets, sems, tiles):
    copies = []
    for step, at in enumerate(tiles):
        copies.append([])
        for number, (source, target) in enumerate(zip(sources, targets)):
            copy = pltpu.make_async_copy(
                source.at[:, at], target.at[:, at], sems.at[number, step]
            )
            copy.start()
            copies[-1].append(copy)
    return copies


def wait_all(copies):
    for copy in copies:
        copy.wait()


def pack(target, hidden, total):
    count, width = hidden.shape
    tiles = tiling(width)

    def body(target_ref, hidden_ref, out_ref, hidden_buf, out_buf, in_sems, out_sems):
        copies = start_all([hidden_ref], [hidden_buf], in_sems, tiles)
        at = lax.broadcasted_iota(jnp.int32, (total, count), 0)
        hot = (at == target_ref[...]).astype(F32).astype(BF16)
        sent = []
        for step, tile in enumerate(tiles):
            wait_all(copies[step])
            out_buf[:, tile] = jnp.dot(
                hot, hidden_buf[:, tile], preferred_element_type=F32
            ).astype(BF16)
            sent.append(
                pltpu.make_async_copy(
                    out_buf.at[:, tile], out_ref.at[:, tile], out_sems.at[0, step]
                )
            )
            sent[-1].start()
        wait_all(sent)

    return call(
        body,
        [(jax.ShapeDtypeStruct((total, width), BF16), True)],
        (target.reshape(1, count), hidden),
        [1],
        [
            pltpu.VMEM((count, width), BF16),
            pltpu.VMEM((total, width), BF16),
            pltpu.SemaphoreType.DMA((1, len(tiles))),
            pltpu.SemaphoreType.DMA((1, len(tiles))),
        ],
        vmem=60,
    )[0]


def unpack(targets, arrays):
    count = targets[0].shape[0]
    width = arrays[0].shape[1]
    tiles = tiling(width)
    kinds = len(arrays)

    def body(*refs):
        target_refs, array_refs, out_ref = refs[:kinds], refs[kinds : 2 * kinds], refs[2 * kinds]
        buffers, out_buf, in_sems, out_sems = refs[2 * kinds + 1 : -3], *refs[-3:]
        copies = start_all(array_refs, buffers, in_sems, tiles)
        hots = []
        for target_ref, array_ref in zip(target_refs, array_refs):
            at = lax.broadcasted_iota(jnp.int32, (count, array_ref.shape[0]), 1)
            hots.append((at == target_ref[...]).astype(F32).astype(BF16))
        sent = []
        for step, tile in enumerate(tiles):
            wait_all(copies[step])
            total = sum(
                jnp.dot(hot, buffer[:, tile], preferred_element_type=F32)
                for hot, buffer in zip(hots, buffers)
            )
            out_buf[:, tile] = total.astype(BF16)
            sent.append(
                pltpu.make_async_copy(
                    out_buf.at[:, tile], out_ref.at[:, tile], out_sems.at[0, step]
                )
            )
            sent[-1].start()
        wait_all(sent)

    return call(
        body,
        [(jax.ShapeDtypeStruct((count, width), BF16), True)],
        (*[target.reshape(count, 1) for target in targets], *arrays),
        range(kinds, 2 * kinds),
        [pltpu.VMEM(array.shape, BF16) for array in arrays]
        + [
            pltpu.VMEM((count, width), BF16),
            pltpu.SemaphoreType.DMA((kinds, len(tiles))),
            pltpu.SemaphoreType.DMA((1, len(tiles))),
        ],
    )[0]


def sketch_weights(down, up):
    layers, width, rank = down.shape
    flat_down = jnp.swapaxes(down, 1, 2).reshape(layers * rank, width)
    return jnp.concatenate([flat_down, up.reshape(layers * rank, width)], axis=0)


def against(left, right):
    return lax.dot_general(left, right, (((1,), (1,)), ((), ())), preferred_element_type=F32)


def gram(weights):
    total, width = weights.shape
    half = total // 2
    tiles = tiling(width)

    def body(weights_ref, out_ref, weights_buf, sems):
        copies = start_all([weights_ref], [weights_buf], sems, tiles)
        for step, tile in enumerate(tiles):
            wait_all(copies[step])
            values = weights_buf[:, tile]
            product = against(values[half:], values)
            out_ref[...] = product if step == 0 else out_ref[...] + product

    return call(
        body,
        [(jax.ShapeDtypeStruct((half, total), F32), False)],
        (weights,),
        [0],
        [pltpu.VMEM((total, width), BF16), pltpu.SemaphoreType.DMA((1, len(tiles)))],
    )[0]


def sketch(rows, weights, rank):
    count, width = rows.shape
    total = weights.shape[0]
    tiles = tiling(width)

    def body(rows_ref, weights_ref, out_ref, narrow_ref, rows_buf, weights_buf, sems):
        copies = start_all([rows_ref, weights_ref], [rows_buf, weights_buf], sems, tiles)
        for step, tile in enumerate(tiles):
            wait_all(copies[step])
            values = rows_buf[:, tile]
            product = against(values, weights_buf[:, tile])
            widened = values.astype(F32)
            squares = jnp.broadcast_to(
                jnp.sum(widened * widened, axis=1, keepdims=True), (count, 128)
            )
            if step == 0:
                out_ref[:, :total] = product
                out_ref[:, total:] = squares
            else:
                out_ref[:, :total] += product
                out_ref[:, total:] += squares
        squares = out_ref[:, total : total + 1]
        column = lax.broadcasted_iota(jnp.int32, (count, total), 1) - (total - rank)
        first = squares.astype(BF16).astype(F32)
        second = (squares - first).astype(BF16).astype(F32)
        third = squares - first - second
        terms = jnp.where(column == 0, first, jnp.where(column == 1, second, third))
        terms = jnp.where(column < 3, terms, 0.0)
        narrow_ref[...] = jnp.where(column < 0, out_ref[:, :total], terms).astype(BF16)

    shape = (count, total + 128)
    return call(
        body,
        [
            (jax.ShapeDtypeStruct(shape, F32), False),
            (jax.ShapeDtypeStruct((count, total), BF16), False),
        ],
        (rows, weights),
        [0, 1],
        [
            pltpu.VMEM((count, width), BF16),
            pltpu.VMEM((total, width), BF16),
            pltpu.SemaphoreType.DMA((2, len(tiles))),
        ],
    )


def sketch_parts(sketched, narrow):
    if lax.axis_size("mp") == 2:
        return [sketched, lax.ppermute(narrow, "mp", [(0, 1), (1, 0)])]
    return [lax.psum(sketched, "mp")]


def widen(part, total, rank):
    if part.dtype == F32:
        return part
    part = part.astype(F32)
    column = lax.broadcasted_iota(jnp.int32, part.shape, 1)
    squares = jnp.sum(jnp.where(column < total - rank, 0.0, part), axis=1, keepdims=True)
    return jnp.concatenate([part, jnp.broadcast_to(squares, (part.shape[0], 128))], 1)


def low_rank(sketched, table, layers, model_width):
    half = table.shape[0]
    total = table.shape[1]
    rank = half // layers
    high = table.astype(BF16)
    rest = (table - high.astype(F32)).astype(BF16)
    projected, overlap = sketched[:, :half], sketched[:, half:total]
    squares = sketched[:, total : total + 1]
    column = lax.broadcasted_iota(jnp.int32, (sketched.shape[0], half), 1)
    low = jnp.zeros((sketched.shape[0], half), F32)
    added = jnp.zeros((sketched.shape[0], total), F32)
    for layer in range(layers):
        here = (column >= layer * rank) & (column < (layer + 1) * rank)
        scaled = (projected + added[:, :half]) * lax.rsqrt(squares / model_width + epsilon)
        scaled = scaled.astype(BF16).astype(F32)
        low = jnp.where(here, scaled, low)
        if layer + 1 < layers:
            narrow = low.astype(BF16)
            after = jnp.dot(narrow, high, preferred_element_type=F32) + jnp.dot(
                narrow, rest, preferred_element_type=F32
            )
            step = 2.0 * overlap + added[:, half:] + after[:, half:]
            change = jnp.sum(jnp.where(here, scaled * step, 0.0), axis=1, keepdims=True)
            squares = jnp.maximum(squares + change, 0.0)
            added = after
    return low.astype(BF16)


def finish(rows, sketched, tables, weights, layers, model_width):
    count, width = rows.shape
    half = weights.shape[0] // 2
    tiles = tiling(width)

    def body(*refs):
        rows_ref, weights_ref = refs[:2]
        sketch_refs = refs[2 : 2 + len(sketched)]
        table_refs = refs[2 + len(sketched) :][: len(tables)]
        out_ref, rows_buf, up_buf, out_buf, in_sems, out_sems = refs[-6:]
        up_ref = weights_ref.at[pl.ds(half, half), :]
        copies = start_all([rows_ref, up_ref], [rows_buf, up_buf], in_sems, tiles)
        whole_sketch = sum(widen(ref[...], 2 * half, half // layers) for ref in sketch_refs)
        whole_table = sum(ref[...] for ref in table_refs)
        low = low_rank(whole_sketch, whole_table, layers, model_width)
        sent = []
        for step, tile in enumerate(tiles):
            wait_all(copies[step])
            update = jnp.dot(low, up_buf[:, tile], preferred_element_type=F32)
            out_buf[:, tile] = (rows_buf[:, tile].astype(F32) + update).astype(BF16)
            sent.append(
                pltpu.make_async_copy(
                    out_buf.at[:, tile], out_ref.at[:, tile], out_sems.at[0, step]
                )
            )
            sent[-1].start()
        wait_all(sent)

    return call(
        body,
        [(jax.ShapeDtypeStruct((count, width), BF16), True)],
        (rows, weights, *sketched, *tables),
        [0, 1],
        [
            pltpu.VMEM((count, width), BF16),
            pltpu.VMEM((half, width), BF16),
            pltpu.VMEM((count, width), BF16),
            pltpu.SemaphoreType.DMA((2, len(tiles))),
            pltpu.SemaphoreType.DMA((1, len(tiles))),
        ],
        vmem=60,
    )[0]


def adapt(rows, weights, tables, layers, model_width):
    rank = weights.shape[0] // (2 * layers)
    sketched = sketch_parts(*sketch(rows, weights, rank))
    return finish(rows, sketched, tables, weights, layers, model_width)


def local(hidden, request_adapter, store_slot, down_store, up_store):
    count, width = hidden.shape
    owners = lax.axis_size("dp")
    adapters = store_slot.shape[0]
    assert adapters == owners and down_store.shape[0] == 1
    layers, rank = down_store.shape[1], down_store.shape[3]
    model_width = width * lax.axis_size("mp")
    slot_rows = count // adapters
    group = 1
    while group * group < owners:
        group *= 2
    planes = owners // group
    me = lax.axis_index("dp")
    my_plane, my_place = me // group, me % group

    adapter_ids = jnp.arange(adapters, dtype=jnp.int32)
    matches = request_adapter[:, None] == adapter_ids[None, :]
    slot = jnp.sum(jnp.where(matches, store_slot[None, :], 0), axis=1)
    request_ids = jnp.arange(count, dtype=jnp.int32)
    earlier = (slot[:, None] == slot[None, :]) & (request_ids[:, None] > request_ids[None, :])
    position = jnp.sum(earlier.astype(jnp.int32), axis=1)
    by_slot = slot[:, None] == adapter_ids[None, :]
    counts = jnp.sum(by_slot.astype(jnp.int32), axis=0)
    over = position >= slot_rows
    excess = jnp.maximum(counts - slot_rows, 0)

    plane = slot // group
    my_choice = jnp.argmax(excess.reshape(planes, group), axis=1).astype(jnp.int32)

    is_mine = jnp.sum(
        jnp.where(adapter_ids[:, None] // group == jnp.arange(planes)[None, :], my_choice, 0), axis=1
    ) == adapter_ids % group
    row_is_mine = jnp.any(by_slot & is_mine[None, :], axis=1)

    def add_over(value, steps):
        pairs = [[(i, i ^ step) for i in range(owners)] for step in steps]
        return value + sum(lax.ppermute(value, "dp", p) for p in pairs)

    def exchange(rows):
        blocks = rows.reshape(owners, slot_rows, width)
        return lax.all_to_all(blocks, "dp", 0, 0, tiled=True).reshape(owners * slot_rows, width)

    target = jnp.where(over, -1, slot * slot_rows + position)
    packed = pack(target, hidden, owners * slot_rows)
    tallies = add_over(jnp.stack([excess, jnp.where(is_mine, 0, excess)]), range(1, group))
    packed, tallies = lax.optimization_barrier((packed, tallies))
    arrived = exchange(packed)

    over_target = jnp.where(
        over & row_is_mine, (plane ^ my_plane) * slot_rows + position - slot_rows, -1
    )
    over_packed = pack(over_target, hidden, planes * slot_rows)

    weights = sketch_weights(down_store[0], up_store[0])
    table = parts_mp(gram(weights))

    plane_excess = tallies[0].reshape(planes, group)
    choice = jnp.argmax(
        lax.dynamic_index_in_dim(plane_excess, my_plane, 0, keepdims=False)
    ).astype(jnp.int32)
    is_choice = adapter_ids == my_plane * group + choice
    tallies = jnp.concatenate([tallies, is_choice.astype(jnp.int32)[None, :]])
    mine = weights
    rows_left = weights.shape[0] // group
    step = 1
    while step < group:
        my_bit = (my_place // step) % 2
        halves = mine.reshape(-1, 2, rows_left, width)
        keep = lax.dynamic_index_in_dim(halves, my_bit, 1, keepdims=False)
        give = lax.dynamic_index_in_dim(halves, 1 - my_bit, 1, keepdims=False)
        taken = lax.ppermute(give, "dp", [(i, i ^ step) for i in range(owners)])
        mine = jnp.where((choice // step) % 2 == my_bit, keep, taken)
        step *= 2
    mine = mine.reshape(rows_left, width)
    mine, tallies = lax.optimization_barrier((mine, tallies))
    tallies = add_over(tallies, range(group, owners, group))

    over_blocks = over_packed.reshape(planes, slot_rows, width)
    over_blocks = [over_blocks[step] for step in range(planes)]

    def to_plane(step, block):
        return lax.ppermute(block, "dp", [(i, i ^ (step * group)) for i in range(owners)])

    over_arrived = [over_blocks[0]] + [to_plane(step, over_blocks[step]) for step in range(1, 2)]
    mine, tallies, arrived, over_arrived, over_blocks, table = lax.optimization_barrier(
        (mine, tallies, arrived, over_arrived, over_blocks, table)
    )

    groups = [[p * group + q for q in range(group)] for p in range(planes)]
    plane_weights = lax.all_gather(mine, "dp", axis_index_groups=groups, tiled=True)

    sketched, narrow = sketch(arrived, weights, rank)
    sketched = sketch_parts(sketched, narrow)
    later = [to_plane(step, over_blocks[step]) for step in range(2, planes)]
    done = finish(arrived, sketched, table, weights, layers, model_width)
    *later, done = lax.optimization_barrier((*later, done))
    over_arrived = over_arrived + later

    returned = [exchange(done)]
    plane_weights, over_arrived[0], done = lax.optimization_barrier(
        (plane_weights, over_arrived[0], done)
    )
    plane_table = parts_mp(gram(plane_weights))
    over_done = adapt(
        jnp.concatenate(over_arrived), plane_weights, plane_table, layers, model_width
    )

    excess, stayed, chosen = tallies
    shared = jnp.argmax(excess * chosen).astype(jnp.int32)

    def back_from(source):
        def moved(rows):
            blocks = rows.reshape(planes, slot_rows, width)
            got = [jnp.where(my_plane == source, blocks[0], jnp.zeros_like(blocks[0]))]
            for step in range(1, planes):
                pairs = [(source * group + q, (source ^ step) * group + q) for q in range(group)]
                got.append(lax.ppermute(blocks[step], "dp", pairs))
            return sum(got)

        return moved

    returned.append(
        lax.switch(shared // group, [back_from(source) for source in range(planes)], over_done)
    )
    over_target = jnp.where(
        over & row_is_mine & (slot == shared), position - slot_rows, -1
    )
    waiting = jnp.where(adapter_ids == shared, stayed, excess) > 0
    targets = [target, over_target]
    result = unpack(targets, returned)

    order = jnp.cumsum(waiting.astype(jnp.int32)) - 1
    rounds = jnp.sum(waiting.astype(jnp.int32))

    def one_round(state):
        at, filled = state
        owner = jnp.sum(jnp.where(waiting & (order == at), adapter_ids, 0))
        own = jnp.where(me == owner, weights, jnp.zeros_like(weights))
        round_weights = lax.psum(own, "dp")
        left = over & (slot == owner) & (over_target < 0)
        target = jnp.where(left, position - slot_rows, -1)
        rows = pack(target, hidden, slot_rows)
        round_table = parts_mp(gram(round_weights))
        done = adapt(rows, round_weights, round_table, layers, model_width)
        back = unpack([target], [done])
        return at + 1, jnp.where((target >= 0)[:, None], back, filled)

    _, result = lax.while_loop(lambda state: state[0] < rounds, one_round, (0, result))
    return result


def solution(mesh):
    return jax.shard_map(
        local,
        mesh=mesh,
        in_specs=(
            P("dp", "mp"),
            P("dp"),
            P(),
            P("dp", None, "mp", None),
            P("dp", None, None, "mp"),
        ),
        out_specs=P("dp", "mp"),
        check_vma=False,
    )
```

```python
import math

import jax
import jax.numpy as jnp
import numpy as np
from jax import lax
from jax.experimental import pallas as pl
from jax.experimental.pallas import tpu as pltpu
from jax.sharding import PartitionSpec as P

epsilon = 1e-05
F32 = jnp.float32
BF16 = jnp.bfloat16


def parts_mp(value):
    size = lax.axis_size("mp")
    if size == 2:
        return [value, lax.ppermute(value, "mp", [(0, 1), (1, 0)])]
    return [lax.psum(value, "mp")]


def tiling(width):
    tile = math.gcd(width, 1024)
    return [pl.ds(step * tile, tile) for step in range(width // tile)]


def call(body, outs, operands, streamed, scratch, vmem=40):
    in_specs = [
        pl.BlockSpec(memory_space=pl.ANY if step in streamed else pltpu.VMEM)
        for step in range(len(operands))
    ]
    out_specs = [
        pl.BlockSpec(memory_space=pltpu.HBM if wide else pltpu.VMEM) for _, wide in outs
    ]
    return pl.pallas_call(
        body,
        out_shape=[out for out, _ in outs],
        in_specs=in_specs,
        out_specs=out_specs,
        scratch_shapes=list(scratch),
        compiler_params=pltpu.CompilerParams(vmem_limit_bytes=vmem * 2**20),
        cost_estimate=pl.CostEstimate(flops=1, bytes_accessed=1, transcendentals=0),
    )(*operands)


def start_all(sources, targets, sems, tiles):
    copies = []
    for step, at in enumerate(tiles):
        copies.append([])
        for number, (source, target) in enumerate(zip(sources, targets)):
            copy = pltpu.make_async_copy(
                source.at[:, at], target.at[:, at], sems.at[number, step]
            )
            copy.start()
            copies[-1].append(copy)
    return copies


def wait_all(copies):
    for copy in copies:
        copy.wait()


def pack(target, hidden, total):
    count, width = hidden.shape
    tiles = tiling(width)

    def body(target_ref, hidden_ref, out_ref, hidden_buf, out_buf, in_sems, out_sems):
        copies = start_all([hidden_ref], [hidden_buf], in_sems, tiles)
        at = lax.broadcasted_iota(jnp.int32, (total, count), 0)
        hot = (at == target_ref[...]).astype(F32).astype(BF16)
        sent = []
        for step, tile in enumerate(tiles):
            wait_all(copies[step])
            out_buf[:, tile] = jnp.dot(
                hot, hidden_buf[:, tile], preferred_element_type=F32
            ).astype(BF16)
            sent.append(
                pltpu.make_async_copy(
                    out_buf.at[:, tile], out_ref.at[:, tile], out_sems.at[0, step]
                )
            )
            sent[-1].start()
        wait_all(sent)

    return call(
        body,
        [(jax.ShapeDtypeStruct((total, width), BF16), True)],
        (target.reshape(1, count), hidden),
        [1],
        [
            pltpu.VMEM((count, width), BF16),
            pltpu.VMEM((total, width), BF16),
            pltpu.SemaphoreType.DMA((1, len(tiles))),
            pltpu.SemaphoreType.DMA((1, len(tiles))),
        ],
        vmem=60,
    )[0]


def unpack(targets, arrays):
    count = targets[0].shape[0]
    width = arrays[0].shape[1]
    tiles = tiling(width)
    kinds = len(arrays)

    def body(*refs):
        target_refs, array_refs, out_ref = refs[:kinds], refs[kinds : 2 * kinds], refs[2 * kinds]
        buffers, out_buf, in_sems, out_sems = refs[2 * kinds + 1 : -3], *refs[-3:]
        copies = start_all(array_refs, buffers, in_sems, tiles)
        hots = []
        for target_ref, array_ref in zip(target_refs, array_refs):
            at = lax.broadcasted_iota(jnp.int32, (count, array_ref.shape[0]), 1)
            hots.append((at == target_ref[...]).astype(F32).astype(BF16))
        sent = []
        for step, tile in enumerate(tiles):
            wait_all(copies[step])
            total = sum(
                jnp.dot(hot, buffer[:, tile], preferred_element_type=F32)
                for hot, buffer in zip(hots, buffers)
            )
            out_buf[:, tile] = total.astype(BF16)
            sent.append(
                pltpu.make_async_copy(
                    out_buf.at[:, tile], out_ref.at[:, tile], out_sems.at[0, step]
                )
            )
            sent[-1].start()
        wait_all(sent)

    return call(
        body,
        [(jax.ShapeDtypeStruct((count, width), BF16), True)],
        (*[target.reshape(count, 1) for target in targets], *arrays),
        range(kinds, 2 * kinds),
        [pltpu.VMEM(array.shape, BF16) for array in arrays]
        + [
            pltpu.VMEM((count, width), BF16),
            pltpu.SemaphoreType.DMA((kinds, len(tiles))),
            pltpu.SemaphoreType.DMA((1, len(tiles))),
        ],
    )[0]


def sketch_weights(down, up):
    layers, width, rank = down.shape
    flat_down = jnp.swapaxes(down, 1, 2).reshape(layers * rank, width)
    return jnp.concatenate([flat_down, up.reshape(layers * rank, width)], axis=0)


def against(left, right):
    return lax.dot_general(left, right, (((1,), (1,)), ((), ())), preferred_element_type=F32)


def gram(weights):
    total, width = weights.shape
    half = total // 2
    tiles = tiling(width)

    def body(weights_ref, out_ref, weights_buf, sems):
        copies = start_all([weights_ref], [weights_buf], sems, tiles)
        for step, tile in enumerate(tiles):
            wait_all(copies[step])
            values = weights_buf[:, tile]
            product = against(values[half:], values)
            out_ref[...] = product if step == 0 else out_ref[...] + product

    return call(
        body,
        [(jax.ShapeDtypeStruct((half, total), F32), False)],
        (weights,),
        [0],
        [pltpu.VMEM((total, width), BF16), pltpu.SemaphoreType.DMA((1, len(tiles)))],
    )[0]


def sketch(rows, weights, rank):
    count, width = rows.shape
    total = weights.shape[0]
    tiles = tiling(width)

    def body(rows_ref, weights_ref, out_ref, narrow_ref, rows_buf, weights_buf, sems):
        copies = start_all([rows_ref, weights_ref], [rows_buf, weights_buf], sems, tiles)
        for step, tile in enumerate(tiles):
            wait_all(copies[step])
            values = rows_buf[:, tile]
            product = against(values, weights_buf[:, tile])
            widened = values.astype(F32)
            squares = jnp.broadcast_to(
                jnp.sum(widened * widened, axis=1, keepdims=True), (count, 128)
            )
            if step == 0:
                out_ref[:, :total] = product
                out_ref[:, total:] = squares
            else:
                out_ref[:, :total] += product
                out_ref[:, total:] += squares
        squares = out_ref[:, total : total + 1]
        column = lax.broadcasted_iota(jnp.int32, (count, total), 1) - (total - rank)
        first = squares.astype(BF16).astype(F32)
        second = (squares - first).astype(BF16).astype(F32)
        third = squares - first - second
        terms = jnp.where(column == 0, first, jnp.where(column == 1, second, third))
        terms = jnp.where(column < 3, terms, 0.0)
        narrow_ref[...] = jnp.where(column < 0, out_ref[:, :total], terms).astype(BF16)

    shape = (count, total + 128)
    return call(
        body,
        [
            (jax.ShapeDtypeStruct(shape, F32), False),
            (jax.ShapeDtypeStruct((count, total), BF16), False),
        ],
        (rows, weights),
        [0, 1],
        [
            pltpu.VMEM((count, width), BF16),
            pltpu.VMEM((total, width), BF16),
            pltpu.SemaphoreType.DMA((2, len(tiles))),
        ],
    )


def sketch_parts(sketched, narrow):
    if lax.axis_size("mp") == 2:
        return [sketched, lax.ppermute(narrow, "mp", [(0, 1), (1, 0)])]
    return [lax.psum(sketched, "mp")]


def widen(part, total, rank):
    if part.dtype == F32:
        return part
    part = part.astype(F32)
    column = lax.broadcasted_iota(jnp.int32, part.shape, 1)
    squares = jnp.sum(jnp.where(column < total - rank, 0.0, part), axis=1, keepdims=True)
    return jnp.concatenate([part, jnp.broadcast_to(squares, (part.shape[0], 128))], 1)


def low_rank(sketched, table, layers, model_width):
    half = table.shape[0]
    total = table.shape[1]
    rank = half // layers
    high = table.astype(BF16)
    rest = (table - high.astype(F32)).astype(BF16)
    projected, overlap = sketched[:, :half], sketched[:, half:total]
    squares = sketched[:, total : total + 1]
    column = lax.broadcasted_iota(jnp.int32, (sketched.shape[0], half), 1)
    low = jnp.zeros((sketched.shape[0], half), F32)
    added = jnp.zeros((sketched.shape[0], total), F32)
    for layer in range(layers):
        here = (column >= layer * rank) & (column < (layer + 1) * rank)
        scaled = (projected + added[:, :half]) * lax.rsqrt(squares / model_width + epsilon)
        scaled = scaled.astype(BF16).astype(F32)
        low = jnp.where(here, scaled, low)
        if layer + 1 < layers:
            narrow = low.astype(BF16)
            after = jnp.dot(narrow, high, preferred_element_type=F32) + jnp.dot(
                narrow, rest, preferred_element_type=F32
            )
            step = 2.0 * overlap + added[:, half:] + after[:, half:]
            change = jnp.sum(jnp.where(here, scaled * step, 0.0), axis=1, keepdims=True)
            squares = jnp.maximum(squares + change, 0.0)
            added = after
    return low.astype(BF16)


def finish(rows, sketched, tables, weights, layers, model_width):
    count, width = rows.shape
    half = weights.shape[0] // 2
    tiles = tiling(width)

    def body(*refs):
        rows_ref, weights_ref = refs[:2]
        sketch_refs = refs[2 : 2 + len(sketched)]
        table_refs = refs[2 + len(sketched) :][: len(tables)]
        out_ref, rows_buf, up_buf, out_buf, in_sems, out_sems = refs[-6:]
        up_ref = weights_ref.at[pl.ds(half, half), :]
        copies = start_all([rows_ref, up_ref], [rows_buf, up_buf], in_sems, tiles)
        whole_sketch = sum(widen(ref[...], 2 * half, half // layers) for ref in sketch_refs)
        whole_table = sum(ref[...] for ref in table_refs)
        low = low_rank(whole_sketch, whole_table, layers, model_width)
        sent = []
        for step, tile in enumerate(tiles):
            wait_all(copies[step])
            update = jnp.dot(low, up_buf[:, tile], preferred_element_type=F32)
            out_buf[:, tile] = (rows_buf[:, tile].astype(F32) + update).astype(BF16)
            sent.append(
                pltpu.make_async_copy(
                    out_buf.at[:, tile], out_ref.at[:, tile], out_sems.at[0, step]
                )
            )
            sent[-1].start()
        wait_all(sent)

    return call(
        body,
        [(jax.ShapeDtypeStruct((count, width), BF16), True)],
        (rows, weights, *sketched, *tables),
        [0, 1],
        [
            pltpu.VMEM((count, width), BF16),
            pltpu.VMEM((half, width), BF16),
            pltpu.VMEM((count, width), BF16),
            pltpu.SemaphoreType.DMA((2, len(tiles))),
            pltpu.SemaphoreType.DMA((1, len(tiles))),
        ],
        vmem=60,
    )[0]


def adapt(rows, weights, tables, layers, model_width):
    rank = weights.shape[0] // (2 * layers)
    sketched = sketch_parts(*sketch(rows, weights, rank))
    return finish(rows, sketched, tables, weights, layers, model_width)


def local(hidden, request_adapter, store_slot, down_store, up_store):
    count, width = hidden.shape
    owners = lax.axis_size("dp")
    adapters = store_slot.shape[0]
    assert adapters == owners and down_store.shape[0] == 1
    layers, rank = down_store.shape[1], down_store.shape[3]
    model_width = width * lax.axis_size("mp")
    slot_rows = count // adapters
    group = 1
    while group * group < owners:
        group *= 2
    planes = owners // group
    me = lax.axis_index("dp")
    my_plane, my_place = me // group, me % group

    adapter_ids = jnp.arange(adapters, dtype=jnp.int32)
    matches = request_adapter[:, None] == adapter_ids[None, :]
    slot = jnp.sum(jnp.where(matches, store_slot[None, :], 0), axis=1)
    request_ids = jnp.arange(count, dtype=jnp.int32)
    earlier = (slot[:, None] == slot[None, :]) & (request_ids[:, None] > request_ids[None, :])
    position = jnp.sum(earlier.astype(jnp.int32), axis=1)
    by_slot = slot[:, None] == adapter_ids[None, :]
    counts = jnp.sum(by_slot.astype(jnp.int32), axis=0)
    over = position >= slot_rows
    excess = jnp.maximum(counts - slot_rows, 0)

    half = max(planes // 2, 1)
    per_half = half * group
    my_choice = jnp.argmax(excess.reshape(-1, per_half), axis=1).astype(jnp.int32)
    is_mine = jnp.any(
        jnp.arange(adapters // per_half)[None, :] * per_half + my_choice[None, :]
        == adapter_ids[:, None],
        axis=1,
    )
    row_is_mine = jnp.any(by_slot & is_mine[None, :], axis=1)

    def add_over(value, steps):
        pairs = [[(i, i ^ step) for i in range(owners)] for step in steps]
        return value + sum(lax.ppermute(value, "dp", p) for p in pairs)

    def exchange(rows):
        blocks = rows.reshape(owners, slot_rows, width)
        return lax.all_to_all(blocks, "dp", 0, 0, tiled=True).reshape(owners * slot_rows, width)

    target = jnp.where(over, -1, slot * slot_rows + position)
    packed = pack(target, hidden, owners * slot_rows)
    tallies = add_over(jnp.stack([excess, jnp.where(is_mine, 0, excess)]), range(1, group))
    packed, tallies = lax.optimization_barrier((packed, tallies))
    arrived = exchange(packed)

    sides = planes // half
    other_side = (slot // per_half != my_plane // half).astype(jnp.int32)
    over_target = jnp.where(over & row_is_mine, other_side * slot_rows + position - slot_rows, -1)
    over_packed = pack(over_target, hidden, sides * slot_rows)

    weights = sketch_weights(down_store[0], up_store[0])
    table = parts_mp(gram(weights))

    plane_excess = tallies[0].reshape(planes, group)
    choice = jnp.argmax(
        lax.dynamic_index_in_dim(plane_excess, my_plane, 0, keepdims=False)
    ).astype(jnp.int32)
    is_choice = adapter_ids == my_plane * group + choice
    tallies = jnp.concatenate([tallies, is_choice.astype(jnp.int32)[None, :]])
    mine = weights
    rows_left = weights.shape[0] // group
    step = 1
    while step < group:
        my_bit = (my_place // step) % 2
        halves = mine.reshape(-1, 2, rows_left, width)
        keep = lax.dynamic_index_in_dim(halves, my_bit, 1, keepdims=False)
        give = lax.dynamic_index_in_dim(halves, 1 - my_bit, 1, keepdims=False)
        taken = lax.ppermute(give, "dp", [(i, i ^ step) for i in range(owners)])
        mine = jnp.where((choice // step) % 2 == my_bit, keep, taken)
        step *= 2
    mine = mine.reshape(rows_left, width)
    mine, tallies = lax.optimization_barrier((mine, tallies))
    tallies = add_over(tallies, range(group, owners, group))

    over_blocks = over_packed.reshape(sides, slot_rows, width)
    over_blocks = [over_blocks[side] for side in range(sides)]

    def to_plane(step, block):
        return lax.ppermute(block, "dp", [(i, i ^ (step * group)) for i in range(owners)])

    def round_half(blocks):
        step = 1
        while step < half:
            blocks = blocks + [to_plane(step, block) for block in blocks]
            step *= 2
        return blocks

    over_arrived = round_half(over_blocks[:1])
    mine, tallies, arrived, over_arrived, over_blocks, table = lax.optimization_barrier(
        (mine, tallies, arrived, over_arrived, over_blocks, table)
    )

    groups = [[p * group + q for q in range(group)] for p in range(planes)]
    plane_weights = lax.all_gather(mine, "dp", axis_index_groups=groups, tiled=True)

    sketched, narrow = sketch(arrived, weights, rank)
    sketched = sketch_parts(sketched, narrow)
    crossed = [to_plane(half, block) for block in over_blocks[1:]]
    crossed, sketched[0] = lax.optimization_barrier((crossed, sketched[0]))
    crossed = round_half(crossed)
    done = finish(arrived, sketched, table, weights, layers, model_width)
    *crossed, done = lax.optimization_barrier((*crossed, done))

    returned = [exchange(done)]
    over_arrived = over_arrived + crossed
    plane_weights, over_arrived[0], done = lax.optimization_barrier(
        (plane_weights, over_arrived[0], done)
    )
    plane_table = parts_mp(gram(plane_weights))
    over_done = adapt(
        jnp.concatenate(over_arrived), plane_weights, plane_table, layers, model_width
    )

    excess, stayed, chosen = tallies
    shared = jnp.argmax(excess * chosen).astype(jnp.int32)

    def back_from(source):
        def moved(rows):
            blocks = rows.reshape(planes, slot_rows, width)
            got = [jnp.where(my_plane == source, blocks[0], jnp.zeros_like(blocks[0]))]
            for step in range(1, planes):
                pairs = [(source * group + q, (source ^ step) * group + q) for q in range(group)]
                got.append(lax.ppermute(blocks[step], "dp", pairs))
            return sum(got)

        return moved

    returned.append(
        lax.switch(shared // group, [back_from(source) for source in range(planes)], over_done)
    )
    over_target = jnp.where(
        over & row_is_mine & (slot == shared), position - slot_rows, -1
    )
    waiting = jnp.where(adapter_ids == shared, stayed, excess) > 0
    targets = [target, over_target]
    result = unpack(targets, returned)

    order = jnp.cumsum(waiting.astype(jnp.int32)) - 1
    rounds = jnp.sum(waiting.astype(jnp.int32))

    def one_round(state):
        at, filled = state
        owner = jnp.sum(jnp.where(waiting & (order == at), adapter_ids, 0))
        own = jnp.where(me == owner, weights, jnp.zeros_like(weights))
        round_weights = lax.psum(own, "dp")
        left = over & (slot == owner) & (over_target < 0)
        target = jnp.where(left, position - slot_rows, -1)
        rows = pack(target, hidden, slot_rows)
        round_table = parts_mp(gram(round_weights))
        done = adapt(rows, round_weights, round_table, layers, model_width)
        back = unpack([target], [done])
        return at + 1, jnp.where((target >= 0)[:, None], back, filled)

    _, result = lax.while_loop(lambda state: state[0] < rounds, one_round, (0, result))
    return result


def solution(mesh):
    return jax.shard_map(
        local,
        mesh=mesh,
        in_specs=(
            P("dp", "mp"),
            P("dp"),
            P(),
            P("dp", None, "mp", None),
            P("dp", None, None, "mp"),
        ),
        out_specs=P("dp", "mp"),
        check_vma=False,
    )
```

```python
import math

import jax
import jax.numpy as jnp
import numpy as np
from jax import lax
from jax.experimental import pallas as pl
from jax.experimental.pallas import tpu as pltpu
from jax.sharding import PartitionSpec as P

epsilon = 1e-05
F32 = jnp.float32
BF16 = jnp.bfloat16


def parts_mp(value):
    size = lax.axis_size("mp")
    if size == 2:
        return [value, lax.ppermute(value, "mp", [(0, 1), (1, 0)])]
    return [lax.psum(value, "mp")]


def tiling(width):
    tile = math.gcd(width, 1024)
    return [pl.ds(step * tile, tile) for step in range(width // tile)]


def call(body, outs, operands, streamed, scratch, vmem=40):
    in_specs = [
        pl.BlockSpec(memory_space=pl.ANY if step in streamed else pltpu.VMEM)
        for step in range(len(operands))
    ]
    out_specs = [
        pl.BlockSpec(memory_space=pltpu.HBM if wide else pltpu.VMEM) for _, wide in outs
    ]
    return pl.pallas_call(
        body,
        out_shape=[out for out, _ in outs],
        in_specs=in_specs,
        out_specs=out_specs,
        scratch_shapes=list(scratch),
        compiler_params=pltpu.CompilerParams(vmem_limit_bytes=vmem * 2**20),
        cost_estimate=pl.CostEstimate(flops=1, bytes_accessed=1, transcendentals=0),
    )(*operands)


def start_all(sources, targets, sems, tiles):
    copies = []
    for step, at in enumerate(tiles):
        copies.append([])
        for number, (source, target) in enumerate(zip(sources, targets)):
            copy = pltpu.make_async_copy(
                source.at[:, at], target.at[:, at], sems.at[number, step]
            )
            copy.start()
            copies[-1].append(copy)
    return copies


def wait_all(copies):
    for copy in copies:
        copy.wait()


def pack(target, hidden, total):
    count, width = hidden.shape
    tiles = tiling(width)

    def body(target_ref, hidden_ref, out_ref, hidden_buf, out_buf, in_sems, out_sems):
        copies = start_all([hidden_ref], [hidden_buf], in_sems, tiles)
        at = lax.broadcasted_iota(jnp.int32, (total, count), 0)
        hot = (at == target_ref[...]).astype(F32).astype(BF16)
        sent = []
        for step, tile in enumerate(tiles):
            wait_all(copies[step])
            out_buf[:, tile] = jnp.dot(
                hot, hidden_buf[:, tile], preferred_element_type=F32
            ).astype(BF16)
            sent.append(
                pltpu.make_async_copy(
                    out_buf.at[:, tile], out_ref.at[:, tile], out_sems.at[0, step]
                )
            )
            sent[-1].start()
        wait_all(sent)

    return call(
        body,
        [(jax.ShapeDtypeStruct((total, width), BF16), True)],
        (target.reshape(1, count), hidden),
        [1],
        [
            pltpu.VMEM((count, width), BF16),
            pltpu.VMEM((total, width), BF16),
            pltpu.SemaphoreType.DMA((1, len(tiles))),
            pltpu.SemaphoreType.DMA((1, len(tiles))),
        ],
        vmem=60,
    )[0]


def unpack(targets, arrays):
    count = targets[0].shape[0]
    width = arrays[0].shape[1]
    tiles = tiling(width)
    kinds = len(arrays)

    def body(*refs):
        target_refs, array_refs, out_ref = refs[:kinds], refs[kinds : 2 * kinds], refs[2 * kinds]
        buffers, out_buf, in_sems, out_sems = refs[2 * kinds + 1 : -3], *refs[-3:]
        copies = start_all(array_refs, buffers, in_sems, tiles)
        hots = []
        for target_ref, array_ref in zip(target_refs, array_refs):
            at = lax.broadcasted_iota(jnp.int32, (count, array_ref.shape[0]), 1)
            hots.append((at == target_ref[...]).astype(F32).astype(BF16))
        sent = []
        for step, tile in enumerate(tiles):
            wait_all(copies[step])
            total = sum(
                jnp.dot(hot, buffer[:, tile], preferred_element_type=F32)
                for hot, buffer in zip(hots, buffers)
            )
            out_buf[:, tile] = total.astype(BF16)
            sent.append(
                pltpu.make_async_copy(
                    out_buf.at[:, tile], out_ref.at[:, tile], out_sems.at[0, step]
                )
            )
            sent[-1].start()
        wait_all(sent)

    return call(
        body,
        [(jax.ShapeDtypeStruct((count, width), BF16), True)],
        (*[target.reshape(count, 1) for target in targets], *arrays),
        range(kinds, 2 * kinds),
        [pltpu.VMEM(array.shape, BF16) for array in arrays]
        + [
            pltpu.VMEM((count, width), BF16),
            pltpu.SemaphoreType.DMA((kinds, len(tiles))),
            pltpu.SemaphoreType.DMA((1, len(tiles))),
        ],
    )[0]


def sketch_weights(down, up):
    layers, width, rank = down.shape
    flat_down = jnp.swapaxes(down, 1, 2).reshape(layers * rank, width)
    return jnp.concatenate([flat_down, up.reshape(layers * rank, width)], axis=0)


def against(left, right):
    return lax.dot_general(left, right, (((1,), (1,)), ((), ())), preferred_element_type=F32)


def gram(weights):
    total, width = weights.shape
    half = total // 2
    tiles = tiling(width)

    def body(weights_ref, out_ref, weights_buf, sems):
        copies = start_all([weights_ref], [weights_buf], sems, tiles)
        for step, tile in enumerate(tiles):
            wait_all(copies[step])
            values = weights_buf[:, tile]
            product = against(values[half:], values)
            out_ref[...] = product if step == 0 else out_ref[...] + product

    return call(
        body,
        [(jax.ShapeDtypeStruct((half, total), F32), False)],
        (weights,),
        [0],
        [pltpu.VMEM((total, width), BF16), pltpu.SemaphoreType.DMA((1, len(tiles)))],
    )[0]


def sketch(rows, weights, rank):
    count, width = rows.shape
    total = weights.shape[0]
    tiles = tiling(width)

    def body(rows_ref, weights_ref, out_ref, narrow_ref, rows_buf, weights_buf, sems):
        copies = start_all([rows_ref, weights_ref], [rows_buf, weights_buf], sems, tiles)
        for step, tile in enumerate(tiles):
            wait_all(copies[step])
            values = rows_buf[:, tile]
            product = against(values, weights_buf[:, tile])
            widened = values.astype(F32)
            squares = jnp.broadcast_to(
                jnp.sum(widened * widened, axis=1, keepdims=True), (count, 128)
            )
            if step == 0:
                out_ref[:, :total] = product
                out_ref[:, total:] = squares
            else:
                out_ref[:, :total] += product
                out_ref[:, total:] += squares
        squares = out_ref[:, total : total + 1]
        column = lax.broadcasted_iota(jnp.int32, (count, total), 1) - (total - rank)
        first = squares.astype(BF16).astype(F32)
        second = (squares - first).astype(BF16).astype(F32)
        third = squares - first - second
        terms = jnp.where(column == 0, first, jnp.where(column == 1, second, third))
        terms = jnp.where(column < 3, terms, 0.0)
        narrow_ref[...] = jnp.where(column < 0, out_ref[:, :total], terms).astype(BF16)

    shape = (count, total + 128)
    return call(
        body,
        [
            (jax.ShapeDtypeStruct(shape, F32), False),
            (jax.ShapeDtypeStruct((count, total), BF16), False),
        ],
        (rows, weights),
        [0, 1],
        [
            pltpu.VMEM((count, width), BF16),
            pltpu.VMEM((total, width), BF16),
            pltpu.SemaphoreType.DMA((2, len(tiles))),
        ],
    )


def sketch_parts(sketched, narrow):
    if lax.axis_size("mp") == 2:
        return [sketched, lax.ppermute(narrow, "mp", [(0, 1), (1, 0)])]
    return [lax.psum(sketched, "mp")]


def widen(part, total, rank):
    if part.dtype == F32:
        return part
    part = part.astype(F32)
    column = lax.broadcasted_iota(jnp.int32, part.shape, 1)
    squares = jnp.sum(jnp.where(column < total - rank, 0.0, part), axis=1, keepdims=True)
    return jnp.concatenate([part, jnp.broadcast_to(squares, (part.shape[0], 128))], 1)


def low_rank(sketched, table, layers, model_width):
    half = table.shape[0]
    total = table.shape[1]
    rank = half // layers
    high = table.astype(BF16)
    rest = (table - high.astype(F32)).astype(BF16)
    projected, overlap = sketched[:, :half], sketched[:, half:total]
    squares = sketched[:, total : total + 1]
    column = lax.broadcasted_iota(jnp.int32, (sketched.shape[0], half), 1)
    low = jnp.zeros((sketched.shape[0], half), F32)
    added = jnp.zeros((sketched.shape[0], total), F32)
    for layer in range(layers):
        here = (column >= layer * rank) & (column < (layer + 1) * rank)
        scaled = (projected + added[:, :half]) * lax.rsqrt(squares / model_width + epsilon)
        scaled = scaled.astype(BF16).astype(F32)
        low = jnp.where(here, scaled, low)
        if layer + 1 < layers:
            narrow = low.astype(BF16)
            after = jnp.dot(narrow, high, preferred_element_type=F32) + jnp.dot(
                narrow, rest, preferred_element_type=F32
            )
            step = 2.0 * overlap + added[:, half:] + after[:, half:]
            change = jnp.sum(jnp.where(here, scaled * step, 0.0), axis=1, keepdims=True)
            squares = jnp.maximum(squares + change, 0.0)
            added = after
    return low.astype(BF16)


def finish(rows, sketched, tables, weights, layers, model_width):
    count, width = rows.shape
    half = weights.shape[0] // 2
    tiles = tiling(width)
    far = [k for k, part in enumerate(sketched) if part.dtype == BF16]

    def body(*refs):
        rows_ref, weights_ref = refs[:2]
        sketch_refs = refs[2 : 2 + len(sketched)]
        table_refs = refs[2 + len(sketched) :][: len(tables)]
        out_ref, rows_buf, up_buf, out_buf, in_sems, out_sems = refs[-6 - 2 * len(far) :][:6]
        landed = {}
        for number, (buffer, sem) in zip(far, [refs[-2:]] if far else []):
            landed[number] = (pltpu.make_async_copy(sketch_refs[number], buffer, sem), buffer)
            landed[number][0].start()
        up_ref = weights_ref.at[pl.ds(half, half), :]
        copies = start_all([rows_ref, up_ref], [rows_buf, up_buf], in_sems, tiles)
        for copy, _ in landed.values():
            copy.wait()
        sketch_refs = [landed[k][1] if k in landed else ref for k, ref in enumerate(sketch_refs)]
        whole_sketch = sum(widen(ref[...], 2 * half, half // layers) for ref in sketch_refs)
        whole_table = sum(ref[...] for ref in table_refs)
        low = low_rank(whole_sketch, whole_table, layers, model_width)
        sent = []
        for step, tile in enumerate(tiles):
            wait_all(copies[step])
            update = jnp.dot(low, up_buf[:, tile], preferred_element_type=F32)
            out_buf[:, tile] = (rows_buf[:, tile].astype(F32) + update).astype(BF16)
            sent.append(
                pltpu.make_async_copy(
                    out_buf.at[:, tile], out_ref.at[:, tile], out_sems.at[0, step]
                )
            )
            sent[-1].start()
        wait_all(sent)

    return call(
        body,
        [(jax.ShapeDtypeStruct((count, width), BF16), True)],
        (rows, weights, *sketched, *tables),
        [0, 1, *[2 + k for k in far]],
        [
            pltpu.VMEM((count, width), BF16),
            pltpu.VMEM((half, width), BF16),
            pltpu.VMEM((count, width), BF16),
            pltpu.SemaphoreType.DMA((2, len(tiles))),
            pltpu.SemaphoreType.DMA((1, len(tiles))),
            *[pltpu.VMEM(sketched[k].shape, BF16) for k in far],
            *[pltpu.SemaphoreType.DMA for _ in far],
        ],
        vmem=60,
    )[0]


def adapt(rows, weights, tables, layers, model_width):
    rank = weights.shape[0] // (2 * layers)
    sketched = sketch_parts(*sketch(rows, weights, rank))
    return finish(rows, sketched, tables, weights, layers, model_width)


def local(hidden, request_adapter, store_slot, down_store, up_store):
    count, width = hidden.shape
    owners = lax.axis_size("dp")
    adapters = store_slot.shape[0]
    assert adapters == owners and down_store.shape[0] == 1
    layers, rank = down_store.shape[1], down_store.shape[3]
    model_width = width * lax.axis_size("mp")
    slot_rows = count // adapters
    group = 1
    while group * group < owners:
        group *= 2
    planes = owners // group
    me = lax.axis_index("dp")
    my_plane, my_place = me // group, me % group

    adapter_ids = jnp.arange(adapters, dtype=jnp.int32)
    matches = request_adapter[:, None] == adapter_ids[None, :]
    slot = jnp.sum(jnp.where(matches, store_slot[None, :], 0), axis=1)
    request_ids = jnp.arange(count, dtype=jnp.int32)
    earlier = (slot[:, None] == slot[None, :]) & (request_ids[:, None] > request_ids[None, :])
    position = jnp.sum(earlier.astype(jnp.int32), axis=1)
    by_slot = slot[:, None] == adapter_ids[None, :]
    counts = jnp.sum(by_slot.astype(jnp.int32), axis=0)
    over = position >= slot_rows
    excess = jnp.maximum(counts - slot_rows, 0)

    half = max(planes // 2, 1)
    per_half = half * group
    my_choice = jnp.argmax(excess.reshape(-1, per_half), axis=1).astype(jnp.int32)
    is_mine = jnp.any(
        jnp.arange(adapters // per_half)[None, :] * per_half + my_choice[None, :]
        == adapter_ids[:, None],
        axis=1,
    )
    row_is_mine = jnp.any(by_slot & is_mine[None, :], axis=1)

    def add_over(value, steps):
        pairs = [[(i, i ^ step) for i in range(owners)] for step in steps]
        return value + sum(lax.ppermute(value, "dp", p) for p in pairs)

    def exchange(rows):
        blocks = rows.reshape(owners, slot_rows, width)
        return lax.all_to_all(blocks, "dp", 0, 0, tiled=True).reshape(owners * slot_rows, width)

    target = jnp.where(over, -1, slot * slot_rows + position)
    packed = pack(target, hidden, owners * slot_rows)
    tallies = add_over(jnp.stack([excess, jnp.where(is_mine, 0, excess)]), range(1, group))
    packed, tallies = lax.optimization_barrier((packed, tallies))
    arrived = exchange(packed)

    sides = planes // half
    other_side = (slot // per_half != my_plane // half).astype(jnp.int32)
    over_target = jnp.where(over & row_is_mine, other_side * slot_rows + position - slot_rows, -1)
    over_packed = pack(over_target, hidden, sides * slot_rows)

    weights = sketch_weights(down_store[0], up_store[0])
    table = parts_mp(gram(weights))

    plane_excess = tallies[0].reshape(planes, group)
    choice = jnp.argmax(
        lax.dynamic_index_in_dim(plane_excess, my_plane, 0, keepdims=False)
    ).astype(jnp.int32)
    is_choice = adapter_ids == my_plane * group + choice
    tallies = jnp.concatenate([tallies, is_choice.astype(jnp.int32)[None, :]])
    mine = weights
    rows_left = weights.shape[0] // group
    step = 1
    while step < group:
        my_bit = (my_place // step) % 2
        halves = mine.reshape(-1, 2, rows_left, width)
        keep = lax.dynamic_index_in_dim(halves, my_bit, 1, keepdims=False)
        give = lax.dynamic_index_in_dim(halves, 1 - my_bit, 1, keepdims=False)
        taken = lax.ppermute(give, "dp", [(i, i ^ step) for i in range(owners)])
        mine = jnp.where((choice // step) % 2 == my_bit, keep, taken)
        step *= 2
    mine = mine.reshape(rows_left, width)
    mine, tallies = lax.optimization_barrier((mine, tallies))
    tallies = add_over(tallies, range(group, owners, group))

    over_blocks = over_packed.reshape(sides, slot_rows, width)
    over_blocks = [over_blocks[side] for side in range(sides)]

    def to_plane(step, block):
        return lax.ppermute(block, "dp", [(i, i ^ (step * group)) for i in range(owners)])

    def round_half(blocks):
        step = 1
        while step < half:
            blocks = blocks + [to_plane(step, block) for block in blocks]
            step *= 2
        return blocks

    over_arrived = round_half(over_blocks[:1])
    mine, tallies, arrived, over_arrived, over_blocks, table = lax.optimization_barrier(
        (mine, tallies, arrived, over_arrived, over_blocks, table)
    )

    groups = [[p * group + q for q in range(group)] for p in range(planes)]
    plane_weights = lax.all_gather(mine, "dp", axis_index_groups=groups, tiled=True)

    sketched, narrow = sketch(arrived, weights, rank)
    sketched = sketch_parts(sketched, narrow)
    crossed = [to_plane(half, block) for block in over_blocks[1:]]
    crossed, sketched[0] = lax.optimization_barrier((crossed, sketched[0]))
    crossed = round_half(crossed)
    done = finish(arrived, sketched, table, weights, layers, model_width)
    *crossed, done = lax.optimization_barrier((*crossed, done))

    returned = [exchange(done)]
    over_arrived = over_arrived + crossed
    plane_weights, over_arrived[0], done = lax.optimization_barrier(
        (plane_weights, over_arrived[0], done)
    )
    plane_table = parts_mp(gram(plane_weights))
    over_done = adapt(
        jnp.concatenate(over_arrived), plane_weights, plane_table, layers, model_width
    )

    excess, stayed, chosen = tallies
    shared = jnp.argmax(excess * chosen).astype(jnp.int32)

    def back_from(source):
        def moved(rows):
            blocks = rows.reshape(planes, slot_rows, width)
            got = [jnp.where(my_plane == source, blocks[0], jnp.zeros_like(blocks[0]))]
            for step in range(1, planes):
                pairs = [(source * group + q, (source ^ step) * group + q) for q in range(group)]
                got.append(lax.ppermute(blocks[step], "dp", pairs))
            return sum(got)

        return moved

    returned.append(
        lax.switch(shared // group, [back_from(source) for source in range(planes)], over_done)
    )
    over_target = jnp.where(
        over & row_is_mine & (slot == shared), position - slot_rows, -1
    )
    waiting = jnp.where(adapter_ids == shared, stayed, excess) > 0
    targets = [target, over_target]
    result = unpack(targets, returned)

    order = jnp.cumsum(waiting.astype(jnp.int32)) - 1
    rounds = jnp.sum(waiting.astype(jnp.int32))

    def one_round(state):
        at, filled = state
        owner = jnp.sum(jnp.where(waiting & (order == at), adapter_ids, 0))
        own = jnp.where(me == owner, weights, jnp.zeros_like(weights))
        round_weights = lax.psum(own, "dp")
        left = over & (slot == owner) & (over_target < 0)
        target = jnp.where(left, position - slot_rows, -1)
        rows = pack(target, hidden, slot_rows)
        round_table = parts_mp(gram(round_weights))
        done = adapt(rows, round_weights, round_table, layers, model_width)
        back = unpack([target], [done])
        return at + 1, jnp.where((target >= 0)[:, None], back, filled)

    _, result = lax.while_loop(lambda state: state[0] < rounds, one_round, (0, result))
    return result


def solution(mesh):
    return jax.shard_map(
        local,
        mesh=mesh,
        in_specs=(
            P("dp", "mp"),
            P("dp"),
            P(),
            P("dp", None, "mp", None),
            P("dp", None, None, "mp"),
        ),
        out_specs=P("dp", "mp"),
        check_vma=False,
    )
```
